128 devices in a mesh: chk: 8 (over x_lo, z), var: 16 (over x_hi, y, core).
Axes of the slice: x: 4 (x_hi: 2, x_lo: 2; x = x_hi * 2 + x_lo), y: 4, z: 4, core: 2. Of those that a mesh axis runs over, the one named last changes fastest.
Arguments:
- tile_bits: int32 [8, 16, 2, 4096], P('chk', 'var'), may hold values 0 or 1
- tile_pos: int32 [8, 16, 2, 2], P('chk', 'var'), may hold values from 0 to 3, as said below
- tile_count: int32 [8, 16], P('chk', 'var'), may hold values from 1 to 2, as said below
- edge_weight: float32 [8, 16, 2, 4096], P('chk', 'var'), may hold values from 0.1 to 1.9
- syndrome: int32 [2048, 128], P('chk'), may hold values 0 or 1
- channel_prior: float32 [4096], P('var'), may hold values from 1 to 6
- out_cot: float32 [4096, 128], P('var'), may hold values from -0.6 to 0.6
Outputs:
- marginals: float32 [4096, 128], P('var')
- weight_grad: float32 [8, 16, 2, 4096], P('chk', 'var')
- prior_grad: float32 [4096], P('var')
The draws below stay inside these ranges and needn't reach their ends.
Inputs may be any that keep to these rules, and one draw needn't show every extreme that they name: `tile_pos`: in each grid cell the 2 slots name distinct tiles of its 4 x 4 block grid, check block first. `tile_count`: some grid cell uses all 2 slots.
All inputs are finite; a program needn't handle non-finite values. No bound on the sum of `tile_bits` or of `syndrome` on one device may be relied on, other than what follows from the above.
Results may differ from the reference program's by a relative error of at most 0.0003.
Values sent between devices are 32-bit elements; how exact they have to be, the bound alone decides.
A program may use at most 256 MiB of HBM per device.

```python
import math
import jax
import jax.numpy as jnp
from jax import lax

TILE = 64
CB_DEV = 4
VB_DEV = 4
TMAX = 2
ITERS = 2
SHOTS = 128
CHECKS = 2048
VARS = 4096
N_CHK = 8
N_VAR = 16


def tile_layout(key):
    base = jax.random.fold_in(key, 29)
    cells = N_CHK * N_VAR
    keys = jax.random.split(jax.random.fold_in(base, 1), cells)

    def one_order(one_key):
        return jax.random.permutation(one_key, CB_DEV * VB_DEV)
    orders = jax.vmap(one_order)(keys).astype(jnp.int32)
    chosen = orders[:, :TMAX]
    positions = jnp.stack([chosen // VB_DEV, chosen % VB_DEV], axis=-1).reshape(N_CHK, N_VAR, TMAX, 2)
    extra = jax.random.randint(jax.random.fold_in(base, 2), (cells,), 0, 4)
    counts = jnp.where(extra == 0, TMAX, 1)
    chosen_cell = jax.random.randint(jax.random.fold_in(base, 3), (), 0, cells)
    counts = jnp.where(jnp.arange(cells) == chosen_cell, TMAX, counts)
    return (positions.astype(jnp.int32), counts.astype(jnp.int32).reshape(N_CHK, N_VAR))


def draw_tile_pos(key, part):
    return tile_layout(key)[0]


def draw_tile_count(key, part):
    return tile_layout(key)[1]


def touch_ends(values, own_key, least, largest):
    longest = values.shape.index(max(values.shape))
    spots = []
    for shift in (0, 1):
        where = [jax.random.randint(jax.random.fold_in(own_key, axis), (), 0, length) for axis, length in enumerate(values.shape)]
        where[longest] = (where[longest] + shift) % values.shape[longest]
        spots.append(tuple(where))
    return values.at[spots[0]].set(least).at[spots[1]].set(largest)


def shard_levels(key, extent, shards, low, largest):
    factor_of = 1.0
    for axis_at, parts in shards:
        steps = jax.random.uniform(jax.random.fold_in(jax.random.fold_in(key, 6), axis_at), (parts,), jnp.float32, low / len(shards), largest / len(shards))
        factor_of = factor_of * jnp.repeat(jnp.exp(steps), extent[axis_at] // parts).reshape((-1,) + (1,) * (len(extent) - 1 - axis_at))
    return factor_of


def bell_draw(key, extent, width, reach, cuts=(), kind=jnp.bfloat16):
    values = jax.random.normal(key, extent, jnp.float32) * width
    if len(cuts) > 0:
        values = shard_levels(key, extent, cuts, -0.22, 0.18) * values
    return jnp.clip(values, min=-reach, max=reach).astype(kind)


def setup_inputs(seed: int = 0) -> dict:
    arg_keys = jax.random.split(jax.random.key(seed), 8)
    tile_bits = touch_ends((jax.random.randint(arg_keys[0], (N_CHK, N_VAR, TMAX, TILE * TILE), 0, 512) < 5).astype(jnp.int32), jax.random.fold_in(arg_keys[0], 1), 0, 1)
    tile_pos = draw_tile_pos(jax.random.fold_in(arg_keys[7], 71), 0)
    tile_count = draw_tile_count(jax.random.fold_in(arg_keys[7], 71), 0)
    edge_weight = jnp.clip(1.0 + 0.18 * jax.random.normal(arg_keys[3], (N_CHK, N_VAR, TMAX, TILE * TILE), jnp.float32), 0.1, 1.9)
    syndrome = touch_ends((jax.random.randint(arg_keys[4], (CHECKS, SHOTS), 0, 4) < 1).astype(jnp.int32), jax.random.fold_in(arg_keys[4], 1), 0, 1)
    channel_prior = jnp.clip(jnp.exp(math.log(6.0) - 1.7917595 * jax.random.uniform(arg_keys[5], (VARS,), jnp.float32) ** shard_levels(arg_keys[5], (VARS,), ((0, 16),), -0.2, 0.2)), 1.0, 6.0)
    out_cot = bell_draw(arg_keys[6], (VARS, SHOTS), 0.1, 0.6, ((0, 16),), jnp.float32)
    return dict(tile_bits=tile_bits, tile_pos=tile_pos, tile_count=tile_count, edge_weight=edge_weight, syndrome=syndrome, channel_prior=channel_prior, out_cot=out_cot)


DAMP = 0.97
EXACT = lax.Precision.HIGHEST

def linear_both(values, axis):
    length = values.shape[axis]
    pieces = [lax.slice_in_dim(values, index, index + 1, axis=axis) for index in range(length)]
    ones = jnp.ones_like(pieces[0])
    prefix = [ones]
    for index in range(length - 1):
        prefix.append(prefix[-1] * pieces[index])
    suffix = [ones]
    for index in range(length - 1, 0, -1):
        suffix.append(suffix[-1] * pieces[index])
    suffix = suffix[::-1]
    whole = prefix[-1] * pieces[-1]
    return (jnp.concatenate(prefix, axis=axis), jnp.concatenate(suffix, axis=axis), whole)

def exclusive_both(values, axis):
    length = values.shape[axis]
    if length < 16 or length % 8 != 0:
        return linear_both(values, axis)
    shape = values.shape
    split = values.reshape(shape[:axis] + (length // 8, 8) + shape[axis + 1:])
    inner_before, inner_after, group_whole = linear_both(split, axis + 1)
    outer_before, outer_after, whole = exclusive_both(group_whole, axis)
    before = (inner_before * outer_before).reshape(shape)
    after = (inner_after * outer_after).reshape(shape)
    whole = whole.reshape(shape[:axis] + (1,) + shape[axis + 1:])
    return (before, after, whole)

def device_tables(bits, positions, count, check_blocks, column_blocks):
    slot_total = bits.shape[0]
    slots = jnp.arange(slot_total, dtype=jnp.int32)
    live = slots < count
    edge = jnp.where(live[:, None], bits, 0).astype(jnp.float32).reshape(slot_total, TILE, TILE)
    row_hot = (positions[:, 0:1] == jnp.arange(check_blocks, dtype=jnp.int32)[None, :]).astype(jnp.float32)
    col_hot = (positions[:, 1:2] == jnp.arange(column_blocks, dtype=jnp.int32)[None, :]).astype(jnp.float32)
    same_row = (positions[:, None, 0] == positions[None, :, 0]) & (slots[:, None] != slots[None, :])
    return (edge, row_hot, col_hot, same_row)

def row_products(messages, edge, row_hot, same_row):
    halves = jnp.where(edge[..., None] > 0, jnp.tanh(0.5 * messages), 1.0)
    before, after, whole = exclusive_both(halves, 2)
    whole = whole[:, :, 0, :]
    rows = jnp.prod(jnp.where(row_hot[:, :, None, None] > 0, whole[:, None], 1.0), axis=0)
    others_here = jnp.prod(jnp.where(same_row[:, :, None, None], whole[None], 1.0), axis=1)
    inner = before * after * others_here[:, :, None, :]
    return (inner, rows)

def edge_messages(inner, others, weight, sign_slot, edge, row_hot, col_hot):
    others_slot = jnp.einsum('kc,crs->krs', row_hot, others, precision=EXACT)
    product = sign_slot[:, :, None, :] * inner * others_slot[:, :, None, :]
    update = (edge * weight)[..., None] * jnp.log((1.0 + DAMP * product) / (1.0 - DAMP * product))
    column = jnp.einsum('kv,kcs->vcs', col_hot, lax.optimization_barrier(jnp.sum(update, axis=1)), precision=EXACT)
    return (update, column)

def reference(tile_bits, tile_pos, tile_count, edge_weight, syndrome, channel_prior, out_cot):

    def tables(bits, positions, count):
        return device_tables(bits, positions, count, CB_DEV, VB_DEV)
    edge, row_hot, col_hot, same_row = jax.vmap(jax.vmap(tables))(tile_bits, tile_pos, tile_count)
    weight = edge_weight.reshape(N_CHK, N_VAR, TMAX, TILE, TILE)
    sign_dev = (1.0 - 2.0 * syndrome.astype(jnp.float32)).reshape(N_CHK, CB_DEV, TILE, SHOTS)
    prior_dev = channel_prior.reshape(N_VAR, VB_DEV, TILE)
    block = math.gcd(SHOTS, 8)
    count_blocks = SHOTS // block
    sign_blocks = jnp.moveaxis(sign_dev.reshape(N_CHK, CB_DEV, TILE, count_blocks, block), 3, 0)
    cot_blocks = jnp.moveaxis(out_cot.reshape(N_VAR, VB_DEV, TILE, count_blocks, block), 3, 0)
    products = jax.vmap(jax.vmap(row_products))
    exchange = jax.vmap(jax.vmap(edge_messages))

    def forward(weight_now, prior_now, sign_block):
        sign_slot = jnp.einsum('ijkc,icrs->ijkrs', row_hot, sign_block, precision=EXACT)
        prior_slot = jnp.einsum('ijkv,jvc->ijkc', col_hot, prior_now, precision=EXACT)
        messages = jnp.broadcast_to(prior_slot[:, :, :, None, :, None], (N_CHK, N_VAR, TMAX, TILE, TILE, block))
        total = None
        for step in range(ITERS):
            inner, rows = products(messages, edge, row_hot, same_row)
            before, after, unused = exclusive_both(rows, 1)
            update, column = exchange(inner, before * after, weight_now, sign_slot, edge, row_hot, col_hot)
            total = prior_now[..., None] + lax.optimization_barrier(jnp.sum(column, axis=0))
            spread = jnp.einsum('ijkv,jvcs->ijkcs', col_hot, total, precision=EXACT)
            messages = spread[:, :, :, None] - update
        return total

    def one_block(carry, pieces):
        sign_block, cot_block = pieces

        def closed(weight_now, prior_now):
            return forward(weight_now, prior_now, sign_block)
        total, pull = jax.vjp(closed, weight, prior_dev)
        weight_part, prior_part = pull(cot_block)
        return ((carry[0] + weight_part, carry[1] + prior_part), total)
    start = (jnp.zeros_like(weight), jnp.zeros_like(prior_dev))
    (weight_grad, prior_grad), totals = lax.scan(one_block, start, (sign_blocks, cot_blocks))
    marginals = jnp.moveaxis(totals, 0, 3).reshape(VARS, SHOTS)
    return (marginals, weight_grad.reshape(N_CHK, N_VAR, TMAX, TILE * TILE), prior_grad.reshape(VARS))
```

```python
import jax
import jax.numpy as jnp
from jax import lax
from jax.experimental import pallas as pl
from jax.experimental.pallas import tpu as pltpu
from jax.sharding import PartitionSpec as P

TILE = 64
ITERS = 2


DAMP = 0.97
EXACT = lax.Precision.HIGHEST


def linear_both(values, axis):
    length = values.shape[axis]
    pieces = [lax.slice_in_dim(values, index, index + 1, axis=axis) for index in range(length)]
    ones = jnp.ones_like(pieces[0])
    prefix = [ones]
    for index in range(length - 1):
        prefix.append(prefix[-1] * pieces[index])
    suffix = [ones]
    for index in range(length - 1, 0, -1):
        suffix.append(suffix[-1] * pieces[index])
    suffix = suffix[::-1]
    whole = prefix[-1] * pieces[-1]
    return (jnp.concatenate(prefix, axis=axis), jnp.concatenate(suffix, axis=axis), whole)


def exclusive_both(values, axis):
    length = values.shape[axis]
    if length < 16 or length % 8 != 0:
        return linear_both(values, axis)
    shape = values.shape
    split = values.reshape(shape[:axis] + (length // 8, 8) + shape[axis + 1 :])
    inner_before, inner_after, group_whole = linear_both(split, axis + 1)
    outer_before, outer_after, whole = exclusive_both(group_whole, axis)
    before = (inner_before * outer_before).reshape(shape)
    after = (inner_after * outer_after).reshape(shape)
    whole = whole.reshape(shape[:axis] + (1,) + shape[axis + 1 :])
    return (before, after, whole)


def device_tables(bits, positions, count, check_blocks, column_blocks):
    slot_total = bits.shape[0]
    slots = jnp.arange(slot_total, dtype=jnp.int32)
    live = slots < count
    edge = jnp.where(live[:, None], bits, 0).astype(jnp.float32).reshape(slot_total, TILE, TILE)
    row_hot = (positions[:, 0:1] == jnp.arange(check_blocks, dtype=jnp.int32)[None, :]).astype(
        jnp.float32
    )
    col_hot = (positions[:, 1:2] == jnp.arange(column_blocks, dtype=jnp.int32)[None, :]).astype(
        jnp.float32
    )
    same_row = (positions[:, None, 0] == positions[None, :, 0]) & (slots[:, None] != slots[None, :])
    return (edge, row_hot, col_hot, same_row)


def row_products(messages, edge, row_hot, same_row):
    halves = jnp.where(edge[..., None] > 0, jnp.tanh(0.5 * messages), 1.0)
    before, after, whole = exclusive_both(halves, 2)
    whole = whole[:, :, 0, :]
    rows = jnp.prod(jnp.where(row_hot[:, :, None, None] > 0, whole[:, None], 1.0), axis=0)
    others_here = jnp.prod(jnp.where(same_row[:, :, None, None], whole[None], 1.0), axis=1)
    inner = before * after * others_here[:, :, None, :]
    return (inner, rows)


def edge_messages(inner, others, weight, sign_slot, edge, row_hot, col_hot):
    others_slot = jnp.einsum("kc,crs->krs", row_hot, others, precision=EXACT)
    product = sign_slot[:, :, None, :] * inner * others_slot[:, :, None, :]
    update = (edge * weight)[..., None] * jnp.log((1.0 + DAMP * product) / (1.0 - DAMP * product))
    column = jnp.einsum("kv,kcs->vcs", col_hot, jnp.sum(update, axis=1), precision=EXACT)
    return (update, column)


def column_sum(values, col_hot):
    return jnp.einsum("kv,kcs->vcs", col_hot, jnp.sum(values, axis=1), precision=EXACT)


def checks_total(values):
    return lax.psum(values, "chk")


def others_forward(rows, check_blocks):
    own = lax.axis_index("var")
    carry = jnp.ones_like(rows)
    piece = jax.tree.map(lambda part: lax.all_gather(part, "var", axis=0, tiled=True), rows)
    indices = jnp.arange(piece.shape[0], dtype=jnp.int32)
    keep = indices // check_blocks != own
    parts = []
    for block in range(check_blocks):
        pick = (keep & (indices % check_blocks == block))[:, None, None]
        parts.append(carry[block] * jnp.prod(jnp.where(pick, piece, 1.0), axis=0))
    others = jnp.stack(parts)
    return (others, (rows, rows))


def others_backward(rows, grads, check_blocks):
    own = lax.axis_index("var")
    kept_products = jnp.ones_like(rows)
    kept_sums = jnp.zeros_like(rows)
    row_piece = lax.all_gather(rows, "var", axis=0, tiled=True)
    grad_piece = lax.all_gather(grads, "var", axis=0, tiled=True)
    indices = jnp.arange(row_piece.shape[0], dtype=jnp.int32)
    keep = indices // check_blocks != own
    new_products = []
    new_sums = []
    for block in range(check_blocks):
        pick = (keep & (indices % check_blocks == block))[:, None, None]
        factors = jnp.where(pick, row_piece, 1.0)
        weights = jnp.where(pick, grad_piece, 0.0)
        before, after, whole = exclusive_both(factors, 0)
        within = jnp.sum(weights * before * after, axis=0)
        whole = whole[0]
        new_sums.append(kept_sums[block] * whole + kept_products[block] * within)
        new_products.append(kept_products[block] * whole)
    return jnp.stack(new_sums)


def dense_body(tile_bits, tile_pos, tile_count, edge_weight, syndrome, channel_prior, out_cot):
    slot_total = tile_bits.shape[2]
    shots = syndrome.shape[1]
    check_blocks = syndrome.shape[0] // TILE
    column_blocks = channel_prior.shape[0] // TILE
    edge, row_hot, col_hot, same_row = device_tables(
        tile_bits[0, 0], tile_pos[0, 0], tile_count[0, 0], check_blocks, column_blocks
    )
    weight = edge_weight[0, 0].reshape(slot_total, TILE, TILE)
    sign_dev = (1.0 - 2.0 * syndrome.astype(jnp.float32)).reshape(check_blocks, TILE, shots)
    sign_slot = jnp.einsum("kc,crs->krs", row_hot, sign_dev, precision=EXACT)
    prior_dev = channel_prior.reshape(column_blocks, TILE)
    prior_slot = jnp.einsum("kv,vc->kc", col_hot, prior_dev, precision=EXACT)
    messages = jnp.broadcast_to(prior_slot[:, None, :, None], (slot_total, TILE, TILE, shots))
    saved = []
    total = None
    for step in range(ITERS):
        inner, rows = row_products(messages, edge, row_hot, same_row)
        others, kept = others_forward(rows, check_blocks)
        update, column = edge_messages(inner, others, weight, sign_slot, edge, row_hot, col_hot)
        total = prior_dev[:, :, None] + lax.psum(column, "chk")
        saved.append((messages, inner, rows, others, kept))
        if step + 1 < ITERS:
            spread = jnp.einsum("kv,vcs->kcs", col_hot, total, precision=EXACT)
            messages = spread[:, None] - update
    marginals = total.reshape(column_blocks * TILE, shots)
    grad_total = out_cot.reshape(column_blocks, TILE, shots)
    grad_update = jnp.zeros((slot_total, TILE, TILE, shots), jnp.float32)
    prior_grad = jnp.zeros((column_blocks, TILE), jnp.float32)
    weight_grad = jnp.zeros_like(weight)
    for step in reversed(range(ITERS)):
        messages_now, inner, rows, others, kept = saved[step]
        prior_grad = prior_grad + jnp.sum(grad_total, axis=2)

        def message_part(inner_now, others_now, weight_now):
            return edge_messages(
                inner_now, others_now, weight_now, sign_slot, edge, row_hot, col_hot
            )

        unused, pull = jax.vjp(message_part, inner, others, weight)
        grad_inner, grad_others, weight_part = pull((grad_update, grad_total))
        weight_grad = weight_grad + weight_part
        grad_rows = others_backward(rows, grad_others, check_blocks)

        def product_part(messages_in):
            return row_products(messages_in, edge, row_hot, same_row)

        unused_rows, pull_rows = jax.vjp(product_part, messages_now)
        grad_messages = pull_rows((grad_inner, grad_rows))[0]
        grad_total = checks_total(column_sum(grad_messages, col_hot))
        grad_update = -grad_messages
    prior_grad = prior_grad + jnp.sum(grad_total, axis=2)
    return (
        marginals,
        weight_grad.reshape(1, 1, slot_total, TILE * TILE),
        prior_grad.reshape(column_blocks * TILE),
    )


EDGES = 128
STEPS = (1, 2, 4, 8)
SPAN = 16
NONE = 300.0
FULL = 1000.0
MESH_ID = pl.DeviceIdType.MESH
F32 = jnp.float32
BF16 = jnp.bfloat16


def iota(shape, axis):
    return lax.broadcasted_iota(jnp.int32, shape, axis)


def take(values, index):
    return jnp.take_along_axis(values, index, axis=1, mode="promise_in_bounds")


def small_dot(left, right, dims):
    return lax.dot_general(
        left.astype(BF16), right.astype(BF16), (dims, ((), ())), preferred_element_type=F32
    )


def exact_dot(left, right, dims):
    return lax.dot_general(
        left, right, (dims, ((), ())), precision=EXACT, preferred_element_type=F32
    )


def edge_list(marks, key_rows, key_lanes):
    ahead = (iota((128, 128), 0) < iota((128, 128), 1)).astype(F32)
    within = small_dot(marks, ahead, ((1,), (0,)))
    counts = small_dot(marks, jnp.ones((128, 128), F32), ((1,), (0,)))
    lower = (key_lanes < key_rows).astype(F32)
    start = small_dot(lower, counts, ((1,), (0,)))
    place = iota((128, 128), 1).astype(F32)
    row_hot = ((place >= start) & (place < start + counts)).astype(F32)
    wanted = jnp.sum(row_hot * (place - start + 1.0), axis=0, keepdims=True)
    ranks = small_dot(marks * (within + 1.0), row_hot, ((0,), (0,)))
    lane_hot = ((ranks == wanted) & (wanted > 0.0)).astype(F32)
    return row_hot, lane_hot, start + within, counts


def unpack_cells(ref, kind):
    return jnp.concatenate(
        [ref[pl.ds(kind * 16 + j, 8, stride=64), :] for j in range(16)], axis=0
    )


def cells(values):
    return [values[j * 8 : j * 8 + 8, :] for j in range(16)]


def spread_rows(rows):
    return jnp.broadcast_to(rows, (16, 8, 128)).reshape(128, 128)


def pick(pair, index, upper):
    return jnp.where(upper, take(pair[1], index), take(pair[0], index))


def last_places(order):
    out = []
    for half in range(2):
        key = (iota((128, 128), 1) + 128 * half).astype(F32)
        place = jnp.zeros((128, 128), jnp.int32)
        seen = jnp.full((128, 128), -1.0, F32)
        for step in (64, 32, 16, 8, 4, 2, 1, 1):
            value = take(order, place + (step - 1))
            fits = value <= key
            place = jnp.where(fits, place + step, place)
            seen = jnp.where(fits, value, seen)
        out.append((jnp.maximum(place - 1, 0), seen == key))
    return out


def back(values, step):
    return pltpu.roll(values, step, 1)


def fore(values, step):
    return pltpu.roll(values, 128 - step, 1)


def scan_products(values, same, shift):
    saved = []
    for step in STEPS:
        before = jnp.where(same[step], shift(values, step), 1.0)
        saved.append((before, values))
        values = before * values
    return values, jnp.where(same[1], shift(values, 1), 1.0), saved


def scan_sums(sums, saved, same, shift):
    for step, (before, values) in zip(STEPS, saved):
        sums = jnp.where(same[step], shift(sums, step), 0.0) * values + before * sums
    return sums, jnp.where(same[1], shift(sums, 1), 0.0)


def cross_products(rows):
    pieces = cells(rows)
    first = [jnp.ones((8, 128), F32)]
    for j in range(15):
        first.append(first[-1] * pieces[j])
    last = [jnp.ones((8, 128), F32)]
    for j in range(15, 0, -1):
        last.append(last[-1] * pieces[j])
    last = last[::-1]
    others = jnp.concatenate([a * b for a, b in zip(first, last)], axis=0)
    return others, (pieces, first, last)


def cross_sums(rows, saved):
    pieces, first, last = saved
    sums = cells(rows)
    first_sum = [jnp.zeros((8, 128), F32)]
    for j in range(15):
        first_sum.append(first_sum[-1] * pieces[j] + first[j] * sums[j])
    last_sum = [jnp.zeros((8, 128), F32)]
    for j in range(15, 0, -1):
        last_sum.append(last_sum[-1] * pieces[j] + last[j] * sums[j])
    last_sum = last_sum[::-1]
    return jnp.concatenate(
        [first_sum[j] * last[j] + first[j] * last_sum[j] for j in range(16)], axis=0
    )


def sparse_kernel(
    count_ref, pos_ref, bits_ref, weight_ref, syndrome_ref, prior_ref, cot_ref,
    marg_ref, wgrad_ref, pgrad_ref, flag_ref,
    raw_bits, raw_weight, row_hot_ref, lane_hot_ref, flip_ref,
    sigma_out, sigma_in, cell_out, cell_in, block_out, block_in,
    part_out, part_in, sum_out, sum_in, send_sem, recv_sem,
):
    i = lax.axis_index("chk")
    j = lax.axis_index("var")
    barrier = pltpu.get_barrier_semaphore()
    for step in range(1, 16):
        pl.semaphore_signal(
            barrier, 1, device_id={"var": lax.rem(j + step, 16)}, device_id_type=MESH_ID
        )
    for step in range(1, 8):
        pl.semaphore_signal(
            barrier, 1, device_id={"chk": lax.rem(i + step, 8)}, device_id_type=MESH_ID
        )

    def send(axis, phase, source, target, rows):
        me, size = (j, 16) if axis == "var" else (i, 8)
        for step in range(1, size):
            other = lax.rem(me + step, size)
            pltpu.make_async_remote_copy(
                src_ref=source(other),
                dst_ref=target.at[pl.ds(pl.multiple_of(me * rows, 8), rows)],
                send_sem=send_sem.at[phase],
                recv_sem=recv_sem.at[phase],
                device_id={axis: other},
                device_id_type=MESH_ID,
            ).start()

    def await_all(sems, phase, target, rows, size):
        whole = target.at[pl.ds(0, rows * (size - 1))]
        pltpu.make_async_copy(whole, whole, sems.at[phase]).wait()

    count = count_ref[0, 0]
    live = (iota((2, 128), 0) < count).astype(F32)
    for m in range(32):
        lanes = pl.ds(m * 128, 128)
        raw_bits[pl.ds(m * 2, 2), :] = bits_ref[0, 0, :, lanes].astype(F32) * live
        raw_weight[pl.ds(m * 2, 2), :] = weight_ref[0, 0, :, lanes]
    narrow = iota((64, 128), 1) < 64

    def entries(ref):
        value = ref[...]
        low = jnp.where(narrow, value, 0.0)
        high = jnp.where(narrow, pltpu.roll(value, 64, 1), 0.0)
        return jnp.concatenate([low, high], axis=0)

    marks = entries(raw_bits)
    weights = entries(raw_weight)
    p0, p1 = pos_ref[0, 0, 0, 0], pos_ref[0, 0, 1, 0]
    q0, q1 = pos_ref[0, 0, 0, 1], pos_ref[0, 0, 1, 1]

    def check_of(axis, shape=(128, 128)):
        at = iota(shape, axis)
        slot = at & 1
        return jnp.where(slot == 0, p0, p1) * 64 + (at & 62) + (at >> 6), slot

    def variable_of(axis):
        at = iota((128, 128), axis)
        slot = at >> 6
        return jnp.where(slot == 0, q0, q1) * 64 + (at & 63), slot

    def unique(pair):
        return pair[0] * 2 + pair[1]

    row_hot, lane_hot, place, counts = edge_list(
        marks, unique(check_of(0)), unique(check_of(1))
    )
    row_hot_ref[...] = row_hot
    lane_hot_ref[...] = lane_hot
    checks, slots = check_of(1, (8, 128))
    columns = jnp.where(slots == 0, q0, q1) * 64
    table = jnp.where(
        iota((8, 128), 0) == 0,
        checks,
        jnp.where(iota((8, 128), 0) == 1, columns, 1),
    ).astype(F32)
    looked = small_dot(table, row_hot, ((1,), (0,)))
    present = looked[2:3, :] > 0.0
    edge_check = jnp.where(present, looked[0:1, :], NONE)
    total_edges = jnp.sum(counts[:, 0:1])
    edge_check = jnp.where(total_edges > EDGES, FULL, edge_check)
    within = iota((128, 128), 0).astype(F32)
    edge_var = looked[1:2, :] + jnp.sum(lane_hot * within, axis=0, keepdims=True)
    weight_at = exact_dot(weights, row_hot, ((0,), (0,)))
    edge_weight = jnp.sum(weight_at * lane_hot, axis=0, keepdims=True)

    def turned(values):
        flipped = jnp.transpose(values)[0:64, :]
        odd = (iota((64, 128), 1) & 1) == 1
        return jnp.concatenate(
            [jnp.where(odd, 0.0, flipped), jnp.where(odd, flipped, 0.0)], axis=0
        )

    marks_turned = turned(marks)
    col_hot, down_hot, unused_place, unused_counts = edge_list(
        marks_turned, unique(variable_of(0)), unique(variable_of(1))
    )
    place_at = small_dot(marks_turned * turned(place), col_hot, ((0,), (0,)))
    order = jnp.sum(place_at * down_hot, axis=0, keepdims=True)

    for half in range(2):
        flip_ref[pl.ds(half * 128, 128), :] = jnp.transpose(
            cot_ref[pl.ds(half * 128, 128), :]
        )
    shots = [
        flip_ref[pl.ds(pl.multiple_of(half * 128 + i * 16, 16), 16), :] for half in range(2)
    ]
    prior_low = prior_ref[pl.ds(0, 128)].reshape(1, 128)
    prior_high = prior_ref[pl.ds(128, 128)].reshape(1, 128)
    fixed = jnp.concatenate(
        [edge_weight, edge_check, edge_var, order, prior_low, prior_high], axis=0
    )
    for t in range(16):
        cell_out[pl.ds(t * 8, 6), :] = fixed
        cell_out[pl.ds(t * 8 + 6, 1), :] = shots[0][t : t + 1, :]
        cell_out[pl.ds(t * 8 + 7, 1), :] = shots[1][t : t + 1, :]
    own = pl.ds(pl.multiple_of(j * 8, 8), 8)
    cell_in[own, :] = cell_out[own, :]
    signs = 1.0 - 2.0 * syndrome_ref[...].astype(F32)
    for half in range(2):
        flip_ref[pl.ds(half * 128, 128), :] = jnp.transpose(
            signs[half * 128 : half * 128 + 128, :]
        )
        sigma_out[pl.ds(half * 8, 8), :] = flip_ref[pl.ds(half * 128 + j, 8, stride=16), :]
    own = pl.ds(pl.multiple_of(i * 16, 16), 16)
    sigma_in[own, :] = sigma_out[...]

    pl.semaphore_wait(barrier, 22)
    send("var", 0, lambda t: cell_out.at[pl.ds(pl.multiple_of(t * 8, 8), 8)], cell_in, 8)
    send("chk", 1, lambda t: sigma_out, sigma_in, 16)
    await_all(recv_sem, 0, cell_in, 8, 16)
    for kind in range(4):
        block_out[pl.ds(kind * 16, 16), :] = cell_in[pl.ds(kind, 16, stride=8), :]
    own = pl.ds(pl.multiple_of(i * 64, 64), 64)
    block_in[own, :] = block_out[...]
    send("chk", 2, lambda t: block_out, block_in, 64)
    await_all(recv_sem, 1, sigma_in, 16, 8)

    def column_rows(kind):
        return cell_in[pl.ds(kind, 16, stride=8), :].reshape(16, 1, 128)

    prior = (column_rows(4), column_rows(5))
    cot = (column_rows(6), column_rows(7))
    sigma = [
        jnp.concatenate([sigma_in[pl.ds(half * 8 + i, 8, stride=16), :]] * 16, axis=0)
        for half in range(2)
    ]
    await_all(recv_sem, 2, block_in, 64, 8)

    weight = unpack_cells(block_in, 0)
    check = unpack_cells(block_in, 1)
    variable = unpack_cells(block_in, 2).astype(jnp.int32)
    order = unpack_cells(block_in, 3).astype(jnp.int32)
    valid = check < 256.0
    check_index = jnp.minimum(check, 255.0).astype(jnp.int32)
    check_upper = check_index >= 128
    check_index = check_index & 127
    var_upper = variable >= 128
    var_index = variable & 127
    by_var = jnp.where(valid, take(variable.astype(F32), order), NONE)
    bad = (
        (check > 500.0)
        | (valid & (check == back(check, SPAN)))
        | (valid & (by_var == back(by_var, SPAN)))
    )
    flag_ref[0, 0] = jnp.max(bad.astype(F32))
    same_back = {step: check == back(check, step) for step in STEPS}
    same_fore = {step: check == fore(check, step) for step in STEPS}
    same_var = {step: by_var == back(by_var, step) for step in STEPS}
    check_last = last_places(check)
    var_last = last_places(by_var)
    sign = pick(sigma, check_index, check_upper)

    def to_edges(rows):
        return pick([spread_rows(rows[0]), spread_rows(rows[1])], var_index, var_upper)

    def to_variables(values):
        values = take(values, order)
        for step in STEPS:
            values = values + jnp.where(same_var[step], back(values, step), 0.0)
        return [
            jnp.sum(
                jnp.where(found, take(values, place), 0.0).reshape(16, 8, 128),
                axis=1,
                keepdims=True,
            )
            for place, found in var_last
        ]

    def exchange(messages):
        halves = jnp.where(valid, jnp.tanh(0.5 * messages), 1.0)
        ahead, before, saved_back = scan_products(halves, same_back, back)
        unused, after, saved_fore = scan_products(halves, same_fore, fore)
        others, saved_cross = [], []
        for place, found in check_last:
            other, kept = cross_products(jnp.where(found, take(ahead, place), 1.0))
            others.append(other)
            saved_cross.append(kept)
        outside = pick(others, check_index, check_upper)
        inner = before * after
        damped = (DAMP * sign) * (inner * outside)
        level = jnp.log((1.0 + damped) / (1.0 - damped))
        saved = (halves, before, after, inner, outside, damped, saved_back, saved_fore, saved_cross)
        return level, saved

    def exchange_grad(grad_update, saved):
        halves, before, after, inner, outside, damped, saved_back, saved_fore, saved_cross = saved
        leaf = grad_update * weight * sign * ((2.0 * DAMP) / (1.0 - damped * damped))
        whole, before_sum = scan_sums(leaf, saved_back, same_back, back)
        unused, after_sum = scan_sums(leaf, saved_fore, same_fore, fore)
        outer = [
            cross_sums(jnp.where(found, take(whole, place), 0.0), kept)
            for (place, found), kept in zip(check_last, saved_cross)
        ]
        outside_sum = pick(outer, check_index, check_upper)
        grad = (before_sum * after + before * after_sum) * outside + inner * outside_sum
        return grad * (0.5 * (1.0 - halves * halves))

    level_one, saved_one = exchange(to_edges(prior))
    update = weight * level_one
    total = [a + b for a, b in zip(prior, to_variables(update))]
    level_two, saved_two = exchange(to_edges(total) - update)
    marginal = [a + b for a, b in zip(prior, to_variables(weight * level_two))]
    edge_cot = to_edges(cot)
    grad_message = exchange_grad(edge_cot, saved_two)
    grad_total = to_variables(grad_message)
    grad_update = to_edges(grad_total) - grad_message
    grad_weight = edge_cot * level_two + grad_update * level_one
    grad_first = to_variables(exchange_grad(grad_update, saved_one))
    grad_prior = [a + b + c for a, b, c in zip(cot, grad_total, grad_first)]

    for half in range(2):
        for t in range(16):
            part_out[pl.ds(t * 16 + half, 1), :] = marginal[half][t]
            part_out[pl.ds(t * 16 + 2 + half, 1), :] = grad_prior[half][t]
    for t in range(16):
        part_out[pl.ds(t * 16 + 8, 8), :] = grad_weight[t * 8 : t * 8 + 8, :]
    own = pl.ds(pl.multiple_of(j * 16, 16), 16)
    part_in[own, :] = part_out[own, :]
    send("var", 3, lambda t: part_out.at[pl.ds(pl.multiple_of(t * 16, 16), 16)], part_in, 16)
    await_all(recv_sem, 3, part_in, 16, 16)
    for half in range(2):
        sum_out[pl.ds(half * 16, 16), :] = part_in[pl.ds(half, 16, stride=16), :]
    weight_sum = part_in[8:16, :]
    for t in range(1, 16):
        weight_sum = weight_sum + part_in[pl.ds(t * 16 + 8, 8), :]
    sum_out[pl.ds(32, 8), :] = weight_sum
    for half in range(2):
        sum_out[pl.ds(40 + half, 1), :] = jnp.sum(
            part_in[pl.ds(2 + half, 16, stride=16), :], axis=0, keepdims=True
        )
    own = pl.ds(pl.multiple_of(i * 48, 16), 48)
    sum_in[own, :] = sum_out[...]
    send("chk", 4, lambda t: sum_out, sum_in, 48)
    await_all(recv_sem, 4, sum_in, 48, 8)
    for half in range(2):
        rows = jnp.concatenate(
            [sum_in[pl.ds(t * 48 + half * 16, 16), :] for t in range(8)], axis=0
        )
        marg_ref[pl.ds(half * 128, 128), :] = jnp.transpose(rows)
        pgrad_ref[pl.ds(half * 128, 128)] = jnp.sum(
            sum_in[pl.ds(40 + half, 8, stride=48), :], axis=0
        )
    edge_grad = jnp.sum(sum_in[pl.ds(32 + i, 8, stride=48), :], axis=0, keepdims=True)
    spread = row_hot_ref[...] * edge_grad
    hot = lane_hot_ref[0:64, :]
    nothing = jnp.zeros((64, 128), F32)
    dense = exact_dot(
        spread[0:64, :], jnp.concatenate([hot, nothing], axis=0), ((1,), (1,))
    ) + exact_dot(spread[64:128, :], jnp.concatenate([nothing, hot], axis=0), ((1,), (1,)))
    for m in range(32):
        wgrad_ref[0, 0, :, pl.ds(m * 128, 128)] = dense[m * 2 : m * 2 + 2, :]

    await_all(send_sem, 0, cell_out, 8, 16)
    await_all(send_sem, 1, sigma_in, 16, 8)
    await_all(send_sem, 2, block_in, 64, 8)
    await_all(send_sem, 3, part_out, 16, 16)
    await_all(send_sem, 4, sum_in, 48, 8)


def sparse_body(tile_bits, tile_pos, tile_count, edge_weight, syndrome, channel_prior, out_cot):
    vmem = pl.BlockSpec(memory_space=pltpu.VMEM)
    smem = pl.BlockSpec(memory_space=pltpu.SMEM)
    shape = jax.ShapeDtypeStruct
    return pl.pallas_call(
        sparse_kernel,
        out_shape=(
            shape(out_cot.shape, F32),
            shape(edge_weight.shape, F32),
            shape(channel_prior.shape, F32),
            shape((1, 1), F32),
        ),
        in_specs=[smem, smem] + [vmem] * 5,
        out_specs=(vmem, vmem, vmem, smem),
        scratch_shapes=[
            pltpu.VMEM((64, 128), F32),
            pltpu.VMEM((64, 128), F32),
            pltpu.VMEM((128, 128), F32),
            pltpu.VMEM((128, 128), F32),
            pltpu.VMEM((256, 128), F32),
            pltpu.VMEM((16, 128), F32),
            pltpu.VMEM((128, 128), F32),
            pltpu.VMEM((128, 128), F32),
            pltpu.VMEM((128, 128), F32),
            pltpu.VMEM((64, 128), F32),
            pltpu.VMEM((512, 128), F32),
            pltpu.VMEM((256, 128), F32),
            pltpu.VMEM((256, 128), F32),
            pltpu.VMEM((48, 128), F32),
            pltpu.VMEM((384, 128), F32),
            pltpu.SemaphoreType.DMA((5,)),
            pltpu.SemaphoreType.DMA((5,)),
        ],
        compiler_params=pltpu.CompilerParams(
            collective_id=0, has_side_effects=True, vmem_limit_bytes=48 << 20
        ),
    )(tile_count, tile_pos, tile_bits, edge_weight, syndrome, channel_prior, out_cot)


def body(*arguments):
    *results, flag = sparse_body(*arguments)
    return lax.cond(
        flag[0, 0] > 0.0,
        lambda given, kept: dense_body(*given),
        lambda given, kept: kept,
        arguments,
        tuple(results),
    )


def solution(mesh):
    placed = (
        P("chk", "var", None, None),
        P("chk", "var", None, None),
        P("chk", "var"),
        P("chk", "var", None, None),
        P("chk", None),
        P("var"),
        P("var", None),
    )
    return jax.shard_map(
        body,
        mesh=mesh,
        in_specs=placed,
        out_specs=(P("var", None), P("chk", "var", None, None), P("var")),
        check_vma=False,
    )
```

```python
import jax
import jax.numpy as jnp
from jax import lax
from jax.experimental import pallas as pl
from jax.experimental.pallas import tpu as pltpu
from jax.sharding import PartitionSpec as P

TILE = 64
ITERS = 2


DAMP = 0.97
EXACT = lax.Precision.HIGHEST


def linear_both(values, axis):
    length = values.shape[axis]
    pieces = [lax.slice_in_dim(values, index, index + 1, axis=axis) for index in range(length)]
    ones = jnp.ones_like(pieces[0])
    prefix = [ones]
    for index in range(length - 1):
        prefix.append(prefix[-1] * pieces[index])
    suffix = [ones]
    for index in range(length - 1, 0, -1):
        suffix.append(suffix[-1] * pieces[index])
    suffix = suffix[::-1]
    whole = prefix[-1] * pieces[-1]
    return (jnp.concatenate(prefix, axis=axis), jnp.concatenate(suffix, axis=axis), whole)


def exclusive_both(values, axis):
    length = values.shape[axis]
    if length < 16 or length % 8 != 0:
        return linear_both(values, axis)
    shape = values.shape
    split = values.reshape(shape[:axis] + (length // 8, 8) + shape[axis + 1 :])
    inner_before, inner_after, group_whole = linear_both(split, axis + 1)
    outer_before, outer_after, whole = exclusive_both(group_whole, axis)
    before = (inner_before * outer_before).reshape(shape)
    after = (inner_after * outer_after).reshape(shape)
    whole = whole.reshape(shape[:axis] + (1,) + shape[axis + 1 :])
    return (before, after, whole)


def device_tables(bits, positions, count, check_blocks, column_blocks):
    slot_total = bits.shape[0]
    slots = jnp.arange(slot_total, dtype=jnp.int32)
    live = slots < count
    edge = jnp.where(live[:, None], bits, 0).astype(jnp.float32).reshape(slot_total, TILE, TILE)
    row_hot = (positions[:, 0:1] == jnp.arange(check_blocks, dtype=jnp.int32)[None, :]).astype(
        jnp.float32
    )
    col_hot = (positions[:, 1:2] == jnp.arange(column_blocks, dtype=jnp.int32)[None, :]).astype(
        jnp.float32
    )
    same_row = (positions[:, None, 0] == positions[None, :, 0]) & (slots[:, None] != slots[None, :])
    return (edge, row_hot, col_hot, same_row)


def row_products(messages, edge, row_hot, same_row):
    halves = jnp.where(edge[..., None] > 0, jnp.tanh(0.5 * messages), 1.0)
    before, after, whole = exclusive_both(halves, 2)
    whole = whole[:, :, 0, :]
    rows = jnp.prod(jnp.where(row_hot[:, :, None, None] > 0, whole[:, None], 1.0), axis=0)
    others_here = jnp.prod(jnp.where(same_row[:, :, None, None], whole[None], 1.0), axis=1)
    inner = before * after * others_here[:, :, None, :]
    return (inner, rows)


def edge_messages(inner, others, weight, sign_slot, edge, row_hot, col_hot):
    others_slot = jnp.einsum("kc,crs->krs", row_hot, others, precision=EXACT)
    product = sign_slot[:, :, None, :] * inner * others_slot[:, :, None, :]
    update = (edge * weight)[..., None] * jnp.log((1.0 + DAMP * product) / (1.0 - DAMP * product))
    column = jnp.einsum("kv,kcs->vcs", col_hot, jnp.sum(update, axis=1), precision=EXACT)
    return (update, column)


def column_sum(values, col_hot):
    return jnp.einsum("kv,kcs->vcs", col_hot, jnp.sum(values, axis=1), precision=EXACT)


def gather_all(values, axis):
    shape = values.shape
    rows = values.size // shape[-1]
    size = lax.axis_size(axis)

    def kernel(given, out, send_sem, recv_sem):
        me = lax.axis_index(axis)
        barrier = pltpu.get_barrier_semaphore()
        for step in range(1, size):
            pl.semaphore_signal(
                barrier,
                1,
                device_id={axis: lax.rem(me + step, size)},
                device_id_type=pl.DeviceIdType.MESH,
            )
        pl.semaphore_wait(barrier, size - 1)
        own = out.at[me]
        for step in range(1, size):
            pltpu.make_async_remote_copy(
                src_ref=given,
                dst_ref=own,
                send_sem=send_sem,
                recv_sem=recv_sem,
                device_id={axis: lax.rem(me + step, size)},
                device_id_type=pl.DeviceIdType.MESH,
            ).start()
        own[...] = given[...]
        whole = out.at[pl.ds(0, size - 1)]
        pltpu.make_async_copy(whole, whole, recv_sem).wait()
        pltpu.make_async_copy(whole, whole, send_sem).wait()

    gathered = pl.pallas_call(
        kernel,
        out_shape=jax.ShapeDtypeStruct((size, rows, shape[-1]), values.dtype),
        in_specs=[pl.BlockSpec(memory_space=pltpu.VMEM)],
        out_specs=pl.BlockSpec(memory_space=pltpu.VMEM),
        scratch_shapes=[pltpu.SemaphoreType.DMA, pltpu.SemaphoreType.DMA],
        compiler_params=pltpu.CompilerParams(
            collective_id=1 if axis == "chk" else 2, has_side_effects=True
        ),
    )(values.reshape(rows, shape[-1]))
    return gathered.reshape((size,) + shape)


def gather_blocks(values):
    return gather_all(values, "var").reshape((-1,) + values.shape[1:])


def checks_total(values):
    return jnp.sum(gather_all(values, "chk"), axis=0)


def others_forward(rows, check_blocks):
    own = lax.axis_index("var")
    carry = jnp.ones_like(rows)
    piece = gather_blocks(rows)
    indices = jnp.arange(piece.shape[0], dtype=jnp.int32)
    keep = indices // check_blocks != own
    parts = []
    for block in range(check_blocks):
        pick = (keep & (indices % check_blocks == block))[:, None, None]
        parts.append(carry[block] * jnp.prod(jnp.where(pick, piece, 1.0), axis=0))
    others = jnp.stack(parts)
    return (others, (rows, rows))


def others_backward(rows, grads, check_blocks):
    own = lax.axis_index("var")
    kept_products = jnp.ones_like(rows)
    kept_sums = jnp.zeros_like(rows)
    row_piece = gather_blocks(rows)
    grad_piece = gather_blocks(grads)
    indices = jnp.arange(row_piece.shape[0], dtype=jnp.int32)
    keep = indices // check_blocks != own
    new_products = []
    new_sums = []
    for block in range(check_blocks):
        pick = (keep & (indices % check_blocks == block))[:, None, None]
        factors = jnp.where(pick, row_piece, 1.0)
        weights = jnp.where(pick, grad_piece, 0.0)
        before, after, whole = exclusive_both(factors, 0)
        within = jnp.sum(weights * before * after, axis=0)
        whole = whole[0]
        new_sums.append(kept_sums[block] * whole + kept_products[block] * within)
        new_products.append(kept_products[block] * whole)
    return jnp.stack(new_sums)


def dense_body(tile_bits, tile_pos, tile_count, edge_weight, syndrome, channel_prior, out_cot):
    slot_total = tile_bits.shape[2]
    shots = syndrome.shape[1]
    check_blocks = syndrome.shape[0] // TILE
    column_blocks = channel_prior.shape[0] // TILE
    edge, row_hot, col_hot, same_row = device_tables(
        tile_bits[0, 0], tile_pos[0, 0], tile_count[0, 0], check_blocks, column_blocks
    )
    weight = edge_weight[0, 0].reshape(slot_total, TILE, TILE)
    sign_dev = (1.0 - 2.0 * syndrome.astype(jnp.float32)).reshape(check_blocks, TILE, shots)
    sign_slot = jnp.einsum("kc,crs->krs", row_hot, sign_dev, precision=EXACT)
    prior_dev = channel_prior.reshape(column_blocks, TILE)
    prior_slot = jnp.einsum("kv,vc->kc", col_hot, prior_dev, precision=EXACT)
    messages = jnp.broadcast_to(prior_slot[:, None, :, None], (slot_total, TILE, TILE, shots))
    saved = []
    total = None
    for step in range(ITERS):
        inner, rows = row_products(messages, edge, row_hot, same_row)
        others, kept = others_forward(rows, check_blocks)
        update, column = edge_messages(inner, others, weight, sign_slot, edge, row_hot, col_hot)
        total = prior_dev[:, :, None] + checks_total(column)
        saved.append((messages, inner, rows, others, kept))
        if step + 1 < ITERS:
            spread = jnp.einsum("kv,vcs->kcs", col_hot, total, precision=EXACT)
            messages = spread[:, None] - update
    marginals = total.reshape(column_blocks * TILE, shots)
    grad_total = out_cot.reshape(column_blocks, TILE, shots)
    grad_update = jnp.zeros((slot_total, TILE, TILE, shots), jnp.float32)
    prior_grad = jnp.zeros((column_blocks, TILE), jnp.float32)
    weight_grad = jnp.zeros_like(weight)
    for step in reversed(range(ITERS)):
        messages_now, inner, rows, others, kept = saved[step]
        prior_grad = prior_grad + jnp.sum(grad_total, axis=2)

        def message_part(inner_now, others_now, weight_now):
            return edge_messages(
                inner_now, others_now, weight_now, sign_slot, edge, row_hot, col_hot
            )

        unused, pull = jax.vjp(message_part, inner, others, weight)
        grad_inner, grad_others, weight_part = pull((grad_update, grad_total))
        weight_grad = weight_grad + weight_part
        grad_rows = others_backward(rows, grad_others, check_blocks)

        def product_part(messages_in):
            return row_products(messages_in, edge, row_hot, same_row)

        unused_rows, pull_rows = jax.vjp(product_part, messages_now)
        grad_messages = pull_rows((grad_inner, grad_rows))[0]
        grad_total = checks_total(column_sum(grad_messages, col_hot))
        grad_update = -grad_messages
    prior_grad = prior_grad + jnp.sum(grad_total, axis=2)
    return (
        marginals,
        weight_grad.reshape(1, 1, slot_total, TILE * TILE),
        prior_grad.reshape(column_blocks * TILE),
    )


EDGES = 128
STEPS = (1, 2, 4, 8)
SPAN = 16
NONE = 300.0
FULL = 1000.0
MESH_ID = pl.DeviceIdType.MESH
F32 = jnp.float32
BF16 = jnp.bfloat16


def iota(shape, axis):
    return lax.broadcasted_iota(jnp.int32, shape, axis)


def take(values, index):
    return jnp.take_along_axis(values, index, axis=1, mode="promise_in_bounds")


def small_dot(left, right, dims):
    return lax.dot_general(
        left.astype(BF16), right.astype(BF16), (dims, ((), ())), preferred_element_type=F32
    )


def exact_dot(left, right, dims):
    return lax.dot_general(
        left, right, (dims, ((), ())), precision=EXACT, preferred_element_type=F32
    )


def edge_list(marks, key_rows, key_lanes):
    ahead = (iota((128, 128), 0) < iota((128, 128), 1)).astype(F32)
    within = small_dot(marks, ahead, ((1,), (0,)))
    counts = small_dot(marks, jnp.ones((128, 128), F32), ((1,), (0,)))
    lower = (key_lanes < key_rows).astype(F32)
    start = small_dot(lower, counts, ((1,), (0,)))
    place = iota((128, 128), 1).astype(F32)
    row_hot = ((place >= start) & (place < start + counts)).astype(F32)
    wanted = jnp.sum(row_hot * (place - start + 1.0), axis=0, keepdims=True)
    ranks = small_dot(marks * (within + 1.0), row_hot, ((0,), (0,)))
    lane_hot = ((ranks == wanted) & (wanted > 0.0)).astype(F32)
    return row_hot, lane_hot, start + within, counts


def unpack_cells(ref, kind):
    return jnp.concatenate(
        [ref[pl.ds(kind * 16 + j, 8, stride=64), :] for j in range(16)], axis=0
    )


def cells(values):
    return [values[j * 8 : j * 8 + 8, :] for j in range(16)]


def spread_rows(rows):
    return jnp.broadcast_to(rows, (16, 8, 128)).reshape(128, 128)


def pick(pair, index, upper):
    return jnp.where(upper, take(pair[1], index), take(pair[0], index))


def last_places(order):
    out = []
    for half in range(2):
        key = (iota((128, 128), 1) + 128 * half).astype(F32)
        place = jnp.zeros((128, 128), jnp.int32)
        seen = jnp.full((128, 128), -1.0, F32)
        for step in (64, 32, 16, 8, 4, 2, 1, 1):
            value = take(order, place + (step - 1))
            fits = value <= key
            place = jnp.where(fits, place + step, place)
            seen = jnp.where(fits, value, seen)
        out.append((jnp.maximum(place - 1, 0), seen == key))
    return out


def back(values, step):
    return pltpu.roll(values, step, 1)


def fore(values, step):
    return pltpu.roll(values, 128 - step, 1)


def scan_products(values, same, shift):
    saved = []
    for step in STEPS:
        before = jnp.where(same[step], shift(values, step), 1.0)
        saved.append((before, values))
        values = before * values
    return values, jnp.where(same[1], shift(values, 1), 1.0), saved


def scan_sums(sums, saved, same, shift):
    for step, (before, values) in zip(STEPS, saved):
        sums = jnp.where(same[step], shift(sums, step), 0.0) * values + before * sums
    return sums, jnp.where(same[1], shift(sums, 1), 0.0)


def cross_products(rows):
    pieces = cells(rows)
    first = [jnp.ones((8, 128), F32)]
    for j in range(15):
        first.append(first[-1] * pieces[j])
    last = [jnp.ones((8, 128), F32)]
    for j in range(15, 0, -1):
        last.append(last[-1] * pieces[j])
    last = last[::-1]
    others = jnp.concatenate([a * b for a, b in zip(first, last)], axis=0)
    return others, (pieces, first, last)


def cross_sums(rows, saved):
    pieces, first, last = saved
    sums = cells(rows)
    first_sum = [jnp.zeros((8, 128), F32)]
    for j in range(15):
        first_sum.append(first_sum[-1] * pieces[j] + first[j] * sums[j])
    last_sum = [jnp.zeros((8, 128), F32)]
    for j in range(15, 0, -1):
        last_sum.append(last_sum[-1] * pieces[j] + last[j] * sums[j])
    last_sum = last_sum[::-1]
    return jnp.concatenate(
        [first_sum[j] * last[j] + first[j] * last_sum[j] for j in range(16)], axis=0
    )


def sparse_kernel(
    count_ref, pos_ref, bits_ref, weight_ref, syndrome_ref, prior_ref, cot_ref,
    sum_in, row_hot_ref, lane_hot_ref, flag_ref,
    raw_bits, raw_weight, flip_ref,
    sigma_out, sigma_in, cell_out, cell_in, block_out, block_in,
    part_out, part_in, sum_out, send_sem, recv_sem,
):
    i = lax.axis_index("chk")
    j = lax.axis_index("var")
    barrier = pltpu.get_barrier_semaphore()
    for step in range(1, 16):
        pl.semaphore_signal(
            barrier, 1, device_id={"var": lax.rem(j + step, 16)}, device_id_type=MESH_ID
        )
    for step in range(1, 8):
        pl.semaphore_signal(
            barrier, 1, device_id={"chk": lax.rem(i + step, 8)}, device_id_type=MESH_ID
        )

    def send(axis, phase, source, target, rows):
        me, size = (j, 16) if axis == "var" else (i, 8)
        for step in range(1, size):
            other = lax.rem(me + step, size)
            pltpu.make_async_remote_copy(
                src_ref=source(other),
                dst_ref=target.at[pl.ds(pl.multiple_of(me * rows, 8), rows)],
                send_sem=send_sem.at[phase],
                recv_sem=recv_sem.at[phase],
                device_id={axis: other},
                device_id_type=MESH_ID,
            ).start()

    def await_all(sems, phase, target, rows, size):
        whole = target.at[pl.ds(0, rows * (size - 1))]
        pltpu.make_async_copy(whole, whole, sems.at[phase]).wait()

    count = count_ref[0, 0]
    live = (iota((2, 128), 0) < count).astype(F32)
    for m in range(32):
        lanes = pl.ds(m * 128, 128)
        raw_bits[pl.ds(m * 2, 2), :] = bits_ref[0, 0, :, lanes].astype(F32) * live
        raw_weight[pl.ds(m * 2, 2), :] = weight_ref[0, 0, :, lanes]
    narrow = iota((64, 128), 1) < 64

    def entries(ref):
        value = ref[...]
        low = jnp.where(narrow, value, 0.0)
        high = jnp.where(narrow, pltpu.roll(value, 64, 1), 0.0)
        return jnp.concatenate([low, high], axis=0)

    marks = entries(raw_bits)
    weights = entries(raw_weight)
    p0, p1 = pos_ref[0, 0, 0, 0], pos_ref[0, 0, 1, 0]
    q0, q1 = pos_ref[0, 0, 0, 1], pos_ref[0, 0, 1, 1]

    def check_of(axis, shape=(128, 128)):
        at = iota(shape, axis)
        slot = at & 1
        return jnp.where(slot == 0, p0, p1) * 64 + (at & 62) + (at >> 6), slot

    def variable_of(axis):
        at = iota((128, 128), axis)
        slot = at >> 6
        return jnp.where(slot == 0, q0, q1) * 64 + (at & 63), slot

    def unique(pair):
        return pair[0] * 2 + pair[1]

    row_hot, lane_hot, place, counts = edge_list(
        marks, unique(check_of(0)), unique(check_of(1))
    )
    row_hot_ref[...] = row_hot
    lane_hot_ref[...] = lane_hot
    checks, slots = check_of(1, (8, 128))
    columns = jnp.where(slots == 0, q0, q1) * 64
    table = jnp.where(
        iota((8, 128), 0) == 0,
        checks,
        jnp.where(iota((8, 128), 0) == 1, columns, 1),
    ).astype(F32)
    looked = small_dot(table, row_hot, ((1,), (0,)))
    present = looked[2:3, :] > 0.0
    edge_check = jnp.where(present, looked[0:1, :], NONE)
    total_edges = jnp.sum(counts[:, 0:1])
    edge_check = jnp.where(total_edges > EDGES, FULL, edge_check)
    within = iota((128, 128), 0).astype(F32)
    edge_var = looked[1:2, :] + jnp.sum(lane_hot * within, axis=0, keepdims=True)
    weight_at = exact_dot(weights, row_hot, ((0,), (0,)))
    edge_weight = jnp.sum(weight_at * lane_hot, axis=0, keepdims=True)

    def turned(values):
        flipped = jnp.transpose(values)[0:64, :]
        odd = (iota((64, 128), 1) & 1) == 1
        return jnp.concatenate(
            [jnp.where(odd, 0.0, flipped), jnp.where(odd, flipped, 0.0)], axis=0
        )

    marks_turned = turned(marks)
    col_hot, down_hot, unused_place, unused_counts = edge_list(
        marks_turned, unique(variable_of(0)), unique(variable_of(1))
    )
    place_at = small_dot(marks_turned * turned(place), col_hot, ((0,), (0,)))
    order = jnp.sum(place_at * down_hot, axis=0, keepdims=True)

    for half in range(2):
        flip_ref[pl.ds(half * 128, 128), :] = jnp.transpose(
            cot_ref[pl.ds(half * 128, 128), :]
        )
    shots = [
        flip_ref[pl.ds(pl.multiple_of(half * 128 + i * 16, 16), 16), :] for half in range(2)
    ]
    prior_low = prior_ref[pl.ds(0, 128)].reshape(1, 128)
    prior_high = prior_ref[pl.ds(128, 128)].reshape(1, 128)
    fixed = jnp.concatenate(
        [edge_weight, edge_check, edge_var, order, prior_low, prior_high], axis=0
    )
    for t in range(16):
        cell_out[pl.ds(t * 8, 6), :] = fixed
        cell_out[pl.ds(t * 8 + 6, 1), :] = shots[0][t : t + 1, :]
        cell_out[pl.ds(t * 8 + 7, 1), :] = shots[1][t : t + 1, :]
    own = pl.ds(pl.multiple_of(j * 8, 8), 8)
    cell_in[own, :] = cell_out[own, :]
    signs = 1.0 - 2.0 * syndrome_ref[...].astype(F32)
    for half in range(2):
        flip_ref[pl.ds(half * 128, 128), :] = jnp.transpose(
            signs[half * 128 : half * 128 + 128, :]
        )
        sigma_out[pl.ds(half * 8, 8), :] = flip_ref[pl.ds(half * 128 + j, 8, stride=16), :]
    own = pl.ds(pl.multiple_of(i * 16, 16), 16)
    sigma_in[own, :] = sigma_out[...]

    pl.semaphore_wait(barrier, 22)
    send("var", 0, lambda t: cell_out.at[pl.ds(pl.multiple_of(t * 8, 8), 8)], cell_in, 8)
    send("chk", 1, lambda t: sigma_out, sigma_in, 16)
    await_all(recv_sem, 0, cell_in, 8, 16)
    for kind in range(4):
        block_out[pl.ds(kind * 16, 16), :] = cell_in[pl.ds(kind, 16, stride=8), :]
    own = pl.ds(pl.multiple_of(i * 64, 64), 64)
    block_in[own, :] = block_out[...]
    send("chk", 2, lambda t: block_out, block_in, 64)
    await_all(recv_sem, 1, sigma_in, 16, 8)

    def column_rows(kind):
        return cell_in[pl.ds(kind, 16, stride=8), :].reshape(16, 1, 128)

    prior = (column_rows(4), column_rows(5))
    cot = (column_rows(6), column_rows(7))
    sigma = [
        jnp.concatenate([sigma_in[pl.ds(half * 8 + i, 8, stride=16), :]] * 16, axis=0)
        for half in range(2)
    ]
    await_all(recv_sem, 2, block_in, 64, 8)

    weight = unpack_cells(block_in, 0)
    check = unpack_cells(block_in, 1)
    variable = unpack_cells(block_in, 2).astype(jnp.int32)
    order = unpack_cells(block_in, 3).astype(jnp.int32)
    valid = check < 256.0
    check_index = jnp.minimum(check, 255.0).astype(jnp.int32)
    check_upper = check_index >= 128
    check_index = check_index & 127
    var_upper = variable >= 128
    var_index = variable & 127
    by_var = jnp.where(valid, take(variable.astype(F32), order), NONE)
    bad = (
        (check > 500.0)
        | (valid & (check == back(check, SPAN)))
        | (valid & (by_var == back(by_var, SPAN)))
    )
    flag_ref[0, 0] = jnp.max(bad.astype(F32))
    same_back = {step: check == back(check, step) for step in STEPS}
    same_fore = {step: check == fore(check, step) for step in STEPS}
    same_var = {step: by_var == back(by_var, step) for step in STEPS}
    check_last = last_places(check)
    var_last = last_places(by_var)
    sign = pick(sigma, check_index, check_upper)

    def to_edges(rows):
        return pick([spread_rows(rows[0]), spread_rows(rows[1])], var_index, var_upper)

    def to_variables(values):
        values = take(values, order)
        for step in STEPS:
            values = values + jnp.where(same_var[step], back(values, step), 0.0)
        return [
            jnp.sum(
                jnp.where(found, take(values, place), 0.0).reshape(16, 8, 128),
                axis=1,
                keepdims=True,
            )
            for place, found in var_last
        ]

    def exchange(messages):
        halves = jnp.where(valid, jnp.tanh(0.5 * messages), 1.0)
        ahead, before, saved_back = scan_products(halves, same_back, back)
        unused, after, saved_fore = scan_products(halves, same_fore, fore)
        others, saved_cross = [], []
        for place, found in check_last:
            other, kept = cross_products(jnp.where(found, take(ahead, place), 1.0))
            others.append(other)
            saved_cross.append(kept)
        outside = pick(others, check_index, check_upper)
        inner = before * after
        damped = (DAMP * sign) * (inner * outside)
        level = jnp.log((1.0 + damped) / (1.0 - damped))
        saved = (halves, before, after, inner, outside, damped, saved_back, saved_fore, saved_cross)
        return level, saved

    def exchange_grad(grad_update, saved):
        halves, before, after, inner, outside, damped, saved_back, saved_fore, saved_cross = saved
        leaf = grad_update * weight * sign * ((2.0 * DAMP) / (1.0 - damped * damped))
        whole, before_sum = scan_sums(leaf, saved_back, same_back, back)
        unused, after_sum = scan_sums(leaf, saved_fore, same_fore, fore)
        outer = [
            cross_sums(jnp.where(found, take(whole, place), 0.0), kept)
            for (place, found), kept in zip(check_last, saved_cross)
        ]
        outside_sum = pick(outer, check_index, check_upper)
        grad = (before_sum * after + before * after_sum) * outside + inner * outside_sum
        return grad * (0.5 * (1.0 - halves * halves))

    level_one, saved_one = exchange(to_edges(prior))
    update = weight * level_one
    total = [a + b for a, b in zip(prior, to_variables(update))]
    level_two, saved_two = exchange(to_edges(total) - update)
    marginal = [a + b for a, b in zip(prior, to_variables(weight * level_two))]
    edge_cot = to_edges(cot)
    grad_message = exchange_grad(edge_cot, saved_two)
    grad_total = to_variables(grad_message)
    grad_update = to_edges(grad_total) - grad_message
    grad_weight = edge_cot * level_two + grad_update * level_one
    grad_first = to_variables(exchange_grad(grad_update, saved_one))
    grad_prior = [a + b + c for a, b, c in zip(cot, grad_total, grad_first)]

    for half in range(2):
        for t in range(16):
            part_out[pl.ds(t * 16 + half, 1), :] = marginal[half][t]
            part_out[pl.ds(t * 16 + 2 + half, 1), :] = grad_prior[half][t]
    for t in range(16):
        part_out[pl.ds(t * 16 + 8, 8), :] = grad_weight[t * 8 : t * 8 + 8, :]
    own = pl.ds(pl.multiple_of(j * 16, 16), 16)
    part_in[own, :] = part_out[own, :]
    send("var", 3, lambda t: part_out.at[pl.ds(pl.multiple_of(t * 16, 16), 16)], part_in, 16)
    await_all(recv_sem, 3, part_in, 16, 16)
    for half in range(2):
        sum_out[pl.ds(half * 16, 16), :] = part_in[pl.ds(half, 16, stride=16), :]
    weight_sum = part_in[8:16, :]
    for t in range(1, 16):
        weight_sum = weight_sum + part_in[pl.ds(t * 16 + 8, 8), :]
    sum_out[pl.ds(32, 8), :] = weight_sum
    for half in range(2):
        sum_out[pl.ds(40 + half, 1), :] = jnp.sum(
            part_in[pl.ds(2 + half, 16, stride=16), :], axis=0, keepdims=True
        )
    own = pl.ds(pl.multiple_of(i * 48, 16), 48)
    sum_in[own, :] = sum_out[...]
    send("chk", 4, lambda t: sum_out, sum_in, 48)
    await_all(recv_sem, 4, sum_in, 48, 8)
    await_all(send_sem, 0, cell_out, 8, 16)
    await_all(send_sem, 1, sigma_in, 16, 8)
    await_all(send_sem, 2, block_in, 64, 8)
    await_all(send_sem, 3, part_out, 16, 16)
    await_all(send_sem, 4, sum_in, 48, 8)


def finish_kernel(sum_in, row_hot_ref, lane_hot_ref, marg_ref, wgrad_ref, pgrad_ref):
    i = lax.axis_index("chk")
    for half in range(2):
        rows = jnp.concatenate(
            [sum_in[pl.ds(t * 48 + half * 16, 16), :] for t in range(8)], axis=0
        )
        marg_ref[pl.ds(half * 128, 128), :] = jnp.transpose(rows)
        pgrad_ref[pl.ds(half * 128, 128)] = jnp.sum(
            sum_in[pl.ds(40 + half, 8, stride=48), :], axis=0
        )
    edge_grad = jnp.sum(sum_in[pl.ds(32 + i, 8, stride=48), :], axis=0, keepdims=True)
    spread = row_hot_ref[...] * edge_grad
    hot = lane_hot_ref[0:64, :]
    nothing = jnp.zeros((64, 128), F32)
    dense = exact_dot(
        spread[0:64, :], jnp.concatenate([hot, nothing], axis=0), ((1,), (1,))
    ) + exact_dot(spread[64:128, :], jnp.concatenate([nothing, hot], axis=0), ((1,), (1,)))
    for m in range(32):
        wgrad_ref[0, 0, :, pl.ds(m * 128, 128)] = dense[m * 2 : m * 2 + 2, :]


VMEM_SPEC = pl.BlockSpec(memory_space=pltpu.VMEM)
SMEM_SPEC = pl.BlockSpec(memory_space=pltpu.SMEM)


def sparse_parts(tile_bits, tile_pos, tile_count, edge_weight, syndrome, channel_prior, out_cot):
    shape = jax.ShapeDtypeStruct
    return pl.pallas_call(
        sparse_kernel,
        out_shape=(
            shape((384, 128), F32),
            shape((128, 128), F32),
            shape((128, 128), F32),
            shape((1, 1), F32),
        ),
        in_specs=[SMEM_SPEC] * 2 + [VMEM_SPEC] * 5,
        out_specs=(VMEM_SPEC, VMEM_SPEC, VMEM_SPEC, SMEM_SPEC),
        scratch_shapes=[
            pltpu.VMEM((64, 128), F32),
            pltpu.VMEM((64, 128), F32),
            pltpu.VMEM((256, 128), F32),
            pltpu.VMEM((16, 128), F32),
            pltpu.VMEM((128, 128), F32),
            pltpu.VMEM((128, 128), F32),
            pltpu.VMEM((128, 128), F32),
            pltpu.VMEM((64, 128), F32),
            pltpu.VMEM((512, 128), F32),
            pltpu.VMEM((256, 128), F32),
            pltpu.VMEM((256, 128), F32),
            pltpu.VMEM((48, 128), F32),
            pltpu.SemaphoreType.DMA((5,)),
            pltpu.SemaphoreType.DMA((5,)),
        ],
        compiler_params=pltpu.CompilerParams(
            collective_id=0, has_side_effects=True, vmem_limit_bytes=48 << 20
        ),
    )(tile_count, tile_pos, tile_bits, edge_weight, syndrome, channel_prior, out_cot)


def finish(parts, row_hot, lane_hot):
    shape = jax.ShapeDtypeStruct
    return pl.pallas_call(
        finish_kernel,
        out_shape=(
            shape((256, 128), F32),
            shape((1, 1, 2, 4096), F32),
            shape((256,), F32),
        ),
        in_specs=[VMEM_SPEC] * 3,
        out_specs=(VMEM_SPEC,) * 3,
    )(parts, row_hot, lane_hot)


def body(*arguments):
    *parts, flag = sparse_parts(*arguments)
    return lax.cond(
        flag[0, 0] > 0.0,
        lambda given, kept: dense_body(*given),
        lambda given, kept: tuple(finish(*kept)),
        arguments,
        tuple(parts),
    )


def solution(mesh):
    placed = (
        P("chk", "var", None, None),
        P("chk", "var", None, None),
        P("chk", "var"),
        P("chk", "var", None, None),
        P("chk", None),
        P("var"),
        P("var", None),
    )
    return jax.shard_map(
        body,
        mesh=mesh,
        in_specs=placed,
        out_specs=(P("var", None), P("chk", "var", None, None), P("var")),
        check_vma=False,
    )
```

```python
import jax
import jax.numpy as jnp
from jax import lax
from jax.experimental import pallas as pl
from jax.experimental.pallas import tpu as pltpu
from jax.sharding import PartitionSpec as P

TILE = 64
ITERS = 2


DAMP = 0.97
EXACT = lax.Precision.HIGHEST


def linear_both(values, axis):
    length = values.shape[axis]
    pieces = [lax.slice_in_dim(values, index, index + 1, axis=axis) for index in range(length)]
    ones = jnp.ones_like(pieces[0])
    prefix = [ones]
    for index in range(length - 1):
        prefix.append(prefix[-1] * pieces[index])
    suffix = [ones]
    for index in range(length - 1, 0, -1):
        suffix.append(suffix[-1] * pieces[index])
    suffix = suffix[::-1]
    whole = prefix[-1] * pieces[-1]
    return (jnp.concatenate(prefix, axis=axis), jnp.concatenate(suffix, axis=axis), whole)


def exclusive_both(values, axis):
    length = values.shape[axis]
    if length < 16 or length % 8 != 0:
        return linear_both(values, axis)
    shape = values.shape
    split = values.reshape(shape[:axis] + (length // 8, 8) + shape[axis + 1 :])
    inner_before, inner_after, group_whole = linear_both(split, axis + 1)
    outer_before, outer_after, whole = exclusive_both(group_whole, axis)
    before = (inner_before * outer_before).reshape(shape)
    after = (inner_after * outer_after).reshape(shape)
    whole = whole.reshape(shape[:axis] + (1,) + shape[axis + 1 :])
    return (before, after, whole)


def device_tables(bits, positions, count, check_blocks, column_blocks):
    slot_total = bits.shape[0]
    slots = jnp.arange(slot_total, dtype=jnp.int32)
    live = slots < count
    edge = jnp.where(live[:, None], bits, 0).astype(jnp.float32).reshape(slot_total, TILE, TILE)
    row_hot = (positions[:, 0:1] == jnp.arange(check_blocks, dtype=jnp.int32)[None, :]).astype(
        jnp.float32
    )
    col_hot = (positions[:, 1:2] == jnp.arange(column_blocks, dtype=jnp.int32)[None, :]).astype(
        jnp.float32
    )
    same_row = (positions[:, None, 0] == positions[None, :, 0]) & (slots[:, None] != slots[None, :])
    return (edge, row_hot, col_hot, same_row)


def row_products(messages, edge, row_hot, same_row):
    halves = jnp.where(edge[..., None] > 0, jnp.tanh(0.5 * messages), 1.0)
    before, after, whole = exclusive_both(halves, 2)
    whole = whole[:, :, 0, :]
    rows = jnp.prod(jnp.where(row_hot[:, :, None, None] > 0, whole[:, None], 1.0), axis=0)
    others_here = jnp.prod(jnp.where(same_row[:, :, None, None], whole[None], 1.0), axis=1)
    inner = before * after * others_here[:, :, None, :]
    return (inner, rows)


def edge_messages(inner, others, weight, sign_slot, edge, row_hot, col_hot):
    others_slot = jnp.einsum("kc,crs->krs", row_hot, others, precision=EXACT)
    product = sign_slot[:, :, None, :] * inner * others_slot[:, :, None, :]
    update = (edge * weight)[..., None] * jnp.log((1.0 + DAMP * product) / (1.0 - DAMP * product))
    column = jnp.einsum("kv,kcs->vcs", col_hot, jnp.sum(update, axis=1), precision=EXACT)
    return (update, column)


def column_sum(values, col_hot):
    return jnp.einsum("kv,kcs->vcs", col_hot, jnp.sum(values, axis=1), precision=EXACT)


def gather_all(values, axis):
    shape = values.shape
    rows = values.size // shape[-1]
    size = lax.axis_size(axis)

    def kernel(given, out, send_sem, recv_sem):
        me = lax.axis_index(axis)
        barrier = pltpu.get_barrier_semaphore()
        for step in range(1, size):
            pl.semaphore_signal(
                barrier,
                1,
                device_id={axis: lax.rem(me + step, size)},
                device_id_type=pl.DeviceIdType.MESH,
            )
        pl.semaphore_wait(barrier, size - 1)
        own = out.at[me]
        for step in range(1, size):
            pltpu.make_async_remote_copy(
                src_ref=given,
                dst_ref=own,
                send_sem=send_sem,
                recv_sem=recv_sem,
                device_id={axis: lax.rem(me + step, size)},
                device_id_type=pl.DeviceIdType.MESH,
            ).start()
        own[...] = given[...]
        whole = out.at[pl.ds(0, size - 1)]
        pltpu.make_async_copy(whole, whole, recv_sem).wait()
        pltpu.make_async_copy(whole, whole, send_sem).wait()

    gathered = pl.pallas_call(
        kernel,
        out_shape=jax.ShapeDtypeStruct((size, rows, shape[-1]), values.dtype),
        in_specs=[pl.BlockSpec(memory_space=pltpu.VMEM)],
        out_specs=pl.BlockSpec(memory_space=pltpu.VMEM),
        scratch_shapes=[pltpu.SemaphoreType.DMA, pltpu.SemaphoreType.DMA],
        compiler_params=pltpu.CompilerParams(
            collective_id=1 if axis == "chk" else 2, has_side_effects=True
        ),
    )(values.reshape(rows, shape[-1]))
    return gathered.reshape((size,) + shape)


def gather_blocks(values):
    return gather_all(values, "var").reshape((-1,) + values.shape[1:])


def checks_total(values):
    return jnp.sum(gather_all(values, "chk"), axis=0)


def others_forward(rows, check_blocks):
    own = lax.axis_index("var")
    carry = jnp.ones_like(rows)
    piece = gather_blocks(rows)
    indices = jnp.arange(piece.shape[0], dtype=jnp.int32)
    keep = indices // check_blocks != own
    parts = []
    for block in range(check_blocks):
        pick = (keep & (indices % check_blocks == block))[:, None, None]
        parts.append(carry[block] * jnp.prod(jnp.where(pick, piece, 1.0), axis=0))
    others = jnp.stack(parts)
    return (others, (rows, rows))


def others_backward(rows, grads, check_blocks):
    own = lax.axis_index("var")
    kept_products = jnp.ones_like(rows)
    kept_sums = jnp.zeros_like(rows)
    row_piece = gather_blocks(rows)
    grad_piece = gather_blocks(grads)
    indices = jnp.arange(row_piece.shape[0], dtype=jnp.int32)
    keep = indices // check_blocks != own
    new_products = []
    new_sums = []
    for block in range(check_blocks):
        pick = (keep & (indices % check_blocks == block))[:, None, None]
        factors = jnp.where(pick, row_piece, 1.0)
        weights = jnp.where(pick, grad_piece, 0.0)
        before, after, whole = exclusive_both(factors, 0)
        within = jnp.sum(weights * before * after, axis=0)
        whole = whole[0]
        new_sums.append(kept_sums[block] * whole + kept_products[block] * within)
        new_products.append(kept_products[block] * whole)
    return jnp.stack(new_sums)


def dense_body(tile_bits, tile_pos, tile_count, edge_weight, syndrome, channel_prior, out_cot):
    slot_total = tile_bits.shape[2]
    shots = syndrome.shape[1]
    check_blocks = syndrome.shape[0] // TILE
    column_blocks = channel_prior.shape[0] // TILE
    edge, row_hot, col_hot, same_row = device_tables(
        tile_bits[0, 0], tile_pos[0, 0], tile_count[0, 0], check_blocks, column_blocks
    )
    weight = edge_weight[0, 0].reshape(slot_total, TILE, TILE)
    sign_dev = (1.0 - 2.0 * syndrome.astype(jnp.float32)).reshape(check_blocks, TILE, shots)
    sign_slot = jnp.einsum("kc,crs->krs", row_hot, sign_dev, precision=EXACT)
    prior_dev = channel_prior.reshape(column_blocks, TILE)
    prior_slot = jnp.einsum("kv,vc->kc", col_hot, prior_dev, precision=EXACT)
    messages = jnp.broadcast_to(prior_slot[:, None, :, None], (slot_total, TILE, TILE, shots))
    saved = []
    total = None
    for step in range(ITERS):
        inner, rows = row_products(messages, edge, row_hot, same_row)
        others, kept = others_forward(rows, check_blocks)
        update, column = edge_messages(inner, others, weight, sign_slot, edge, row_hot, col_hot)
        total = prior_dev[:, :, None] + checks_total(column)
        saved.append((messages, inner, rows, others, kept))
        if step + 1 < ITERS:
            spread = jnp.einsum("kv,vcs->kcs", col_hot, total, precision=EXACT)
            messages = spread[:, None] - update
    marginals = total.reshape(column_blocks * TILE, shots)
    grad_total = out_cot.reshape(column_blocks, TILE, shots)
    grad_update = jnp.zeros((slot_total, TILE, TILE, shots), jnp.float32)
    prior_grad = jnp.zeros((column_blocks, TILE), jnp.float32)
    weight_grad = jnp.zeros_like(weight)
    for step in reversed(range(ITERS)):
        messages_now, inner, rows, others, kept = saved[step]
        prior_grad = prior_grad + jnp.sum(grad_total, axis=2)

        def message_part(inner_now, others_now, weight_now):
            return edge_messages(
                inner_now, others_now, weight_now, sign_slot, edge, row_hot, col_hot
            )

        unused, pull = jax.vjp(message_part, inner, others, weight)
        grad_inner, grad_others, weight_part = pull((grad_update, grad_total))
        weight_grad = weight_grad + weight_part
        grad_rows = others_backward(rows, grad_others, check_blocks)

        def product_part(messages_in):
            return row_products(messages_in, edge, row_hot, same_row)

        unused_rows, pull_rows = jax.vjp(product_part, messages_now)
        grad_messages = pull_rows((grad_inner, grad_rows))[0]
        grad_total = checks_total(column_sum(grad_messages, col_hot))
        grad_update = -grad_messages
    prior_grad = prior_grad + jnp.sum(grad_total, axis=2)
    return (
        marginals,
        weight_grad.reshape(1, 1, slot_total, TILE * TILE),
        prior_grad.reshape(column_blocks * TILE),
    )


EDGES = 128
NEAR = (1, 2)
FAR = (1, 4, 7)
VAR_FAR = (3, 6, 9)
CHECK_SPAN = 10
VAR_SPAN = 12
NONE = 300.0
FULL = 1000.0
MESH_ID = pl.DeviceIdType.MESH
F32 = jnp.float32
BF16 = jnp.bfloat16


def iota(shape, axis):
    return lax.broadcasted_iota(jnp.int32, shape, axis)


def take(values, index):
    return jnp.take_along_axis(values, index, axis=1, mode="promise_in_bounds")


def small_dot(left, right, dims):
    return lax.dot_general(
        left.astype(BF16), right.astype(BF16), (dims, ((), ())), preferred_element_type=F32
    )


def exact_dot(left, right, dims):
    return lax.dot_general(
        left, right, (dims, ((), ())), precision=EXACT, preferred_element_type=F32
    )


def edge_list(marks, key_rows, key_lanes):
    ahead = (iota((128, 128), 0) < iota((128, 128), 1)).astype(F32)
    within = small_dot(marks, ahead, ((1,), (0,)))
    counts = small_dot(marks, jnp.ones((128, 128), F32), ((1,), (0,)))
    lower = (key_lanes < key_rows).astype(F32)
    start = small_dot(lower, counts, ((1,), (0,)))
    place = iota((128, 128), 1).astype(F32)
    row_hot = ((place >= start) & (place < start + counts)).astype(F32)
    wanted = jnp.sum(row_hot * (place - start + 1.0), axis=0, keepdims=True)
    ranks = small_dot(marks * (within + 1.0), row_hot, ((0,), (0,)))
    lane_hot = ((ranks == wanted) & (wanted > 0.0)).astype(F32)
    return row_hot, lane_hot, start + within, counts


def cells(values):
    return [values[j * 8 : j * 8 + 8, :] for j in range(16)]


def spread_rows(rows):
    return jnp.broadcast_to(rows, (16, 8, 128)).reshape(128, 128)


def pick(pair, index, upper):
    return jnp.where(upper, take(pair[1], index), take(pair[0], index))


def last_places(order):
    out = []
    for half in range(2):
        key = (iota((128, 128), 1) + 128 * half).astype(F32)
        place = jnp.zeros((128, 128), jnp.int32)
        seen = jnp.full((128, 128), -1.0, F32)
        for step in (64, 32, 16, 8, 4, 2, 1, 1):
            value = take(order, place + (step - 1))
            fits = value <= key
            place = jnp.where(fits, place + step, place)
            seen = jnp.where(fits, value, seen)
        out.append((jnp.maximum(place - 1, 0), seen == key))
    return out


def back(values, step):
    return pltpu.roll(values, step, 1)


def fore(values, step):
    return pltpu.roll(values, 128 - step, 1)


def scan_products(values, same, shift):
    one, two = (jnp.where(same[step], shift(values, step), 1.0) for step in NEAR)
    group = values * one * two
    far = [jnp.where(same[step], shift(group, step), 1.0) for step in FAR]
    return far[0] * far[1] * far[2], (values, one, two, far)


def scan_sums(sums, saved, same, shift):
    values, one, two, far = saved
    one_sum, two_sum = (jnp.where(same[step], shift(sums, step), 0.0) for step in NEAR)
    group = (sums * one + values * one_sum) * two + (values * one) * two_sum
    a, b, c = (jnp.where(same[step], shift(group, step), 0.0) for step in FAR)
    return (a * far[1] + far[0] * b) * far[2] + (far[0] * far[1]) * c


def cross_products(rows):
    pieces = cells(rows)
    first = [jnp.ones((8, 128), F32)]
    for j in range(15):
        first.append(first[-1] * pieces[j])
    last = [jnp.ones((8, 128), F32)]
    for j in range(15, 0, -1):
        last.append(last[-1] * pieces[j])
    last = last[::-1]
    others = jnp.concatenate([a * b for a, b in zip(first, last)], axis=0)
    return others, (pieces, first, last)


def cross_sums(rows, saved):
    pieces, first, last = saved
    sums = cells(rows)
    first_sum = [jnp.zeros((8, 128), F32)]
    for j in range(15):
        first_sum.append(first_sum[-1] * pieces[j] + first[j] * sums[j])
    last_sum = [jnp.zeros((8, 128), F32)]
    for j in range(15, 0, -1):
        last_sum.append(last_sum[-1] * pieces[j] + last[j] * sums[j])
    last_sum = last_sum[::-1]
    return jnp.concatenate(
        [first_sum[j] * last[j] + first[j] * last_sum[j] for j in range(16)], axis=0
    )


def sparse_kernel(
    count_hbm, pos_hbm, bits_hbm, weight_hbm, syndrome_hbm, prior_hbm, cot_hbm,
    marg_ref, wgrad_ref, pgrad_ref, flag_ref,
    count_ref, pos_ref, bits_ref, weight_ref, syndrome_ref, prior_ref, cot_ref, load_sem,
    raw_bits, raw_weight, row_hot_ref, lane_hot_ref, flip_ref,
    cell_out, cell_in, prior_out, prior_in, sigma_out, sigma_in, cot_out, cot_in,
    marg_out, marg_in, weight_out, weight_in, late_out, late_in,
    size_1, size_2, size_4, entered, send_sem, recv_sem,
):
    row_sizes = {1: size_1, 2: size_2, 4: size_4}
    i = lax.axis_index("chk")
    j = lax.axis_index("var")
    barrier = pltpu.get_barrier_semaphore()
    for step in range(1, 16):
        pl.semaphore_signal(
            barrier, 1, device_id={"var": lax.rem(j + step, 16)}, device_id_type=MESH_ID
        )
    for step in range(1, 8):
        pl.semaphore_signal(
            barrier, 1, device_id={"chk": lax.rem(i + step, 8)}, device_id_type=MESH_ID
        )
    loads = [
        pltpu.make_async_copy(given, held, load_sem.at[at])
        for at, (given, held) in enumerate(
            (
                (count_hbm, count_ref),
                (pos_hbm, pos_ref),
                (bits_hbm, bits_ref),
                (weight_hbm, weight_ref),
                (prior_hbm, prior_ref),
                (cot_hbm, cot_ref),
                (syndrome_hbm, syndrome_ref),
            )
        )
    ]
    for load in loads:
        load.start()

    def send(phase, source, target, row, turn):
        pltpu.make_async_remote_copy(
            src_ref=source,
            dst_ref=target.at[pl.ds(row, 1)],
            send_sem=send_sem.at[phase],
            recv_sem=recv_sem.at[phase],
            device_id={
                "chk": lax.bitwise_xor(i, turn // 16),
                "var": lax.bitwise_xor(j, turn % 16),
            },
            device_id_type=MESH_ID,
        ).start()

    everyone = sorted(range(1, 128), key=lambda turn: -bin(turn).count("1"))
    of_row = [turn for turn in everyone if turn < 16]
    of_column = [turn for turn in everyone if turn % 16 == 0]

    def wait_for(sems, phase, target, count):
        whole = row_sizes[target.shape[1] // 128].at[pl.ds(0, count)]
        pltpu.make_async_copy(whole, whole, sems.at[phase]).wait()

    for load in loads[0:4]:
        load.wait()
    count = count_ref[0, 0]
    live = (iota((2, 128), 0) < count).astype(F32)
    for m in range(32):
        lanes = pl.ds(m * 128, 128)
        raw_bits[pl.ds(m * 2, 2), :] = bits_ref[0, 0, :, lanes].astype(F32) * live
        raw_weight[pl.ds(m * 2, 2), :] = weight_ref[0, 0, :, lanes]
    narrow = iota((64, 128), 1) < 64

    def entries(ref):
        value = ref[...]
        low = jnp.where(narrow, value, 0.0)
        high = jnp.where(narrow, pltpu.roll(value, 64, 1), 0.0)
        return jnp.concatenate([low, high], axis=0)

    marks = entries(raw_bits)
    weights = entries(raw_weight)
    p0, p1 = pos_ref[0, 0, 0, 0], pos_ref[0, 0, 1, 0]
    q0, q1 = pos_ref[0, 0, 0, 1], pos_ref[0, 0, 1, 1]

    def check_of(axis, shape=(128, 128)):
        at = iota(shape, axis)
        slot = at & 1
        return jnp.where(slot == 0, p0, p1) * 64 + (at & 62) + (at >> 6), slot

    def variable_of(axis):
        at = iota((128, 128), axis)
        slot = at >> 6
        return jnp.where(slot == 0, q0, q1) * 64 + (at & 63), slot

    def unique(pair):
        return pair[0] * 2 + pair[1]

    row_hot, lane_hot, place, counts = edge_list(
        marks, unique(check_of(0)), unique(check_of(1))
    )
    row_hot_ref[...] = row_hot
    lane_hot_ref[...] = lane_hot
    checks, slots = check_of(1, (8, 128))
    columns = jnp.where(slots == 0, q0, q1) * 64
    table = jnp.where(
        iota((8, 128), 0) == 0,
        checks,
        jnp.where(iota((8, 128), 0) == 1, columns, 1),
    ).astype(F32)
    looked = small_dot(table, row_hot, ((1,), (0,)))
    present = looked[2:3, :] > 0.0
    edge_check = jnp.where(present, looked[0:1, :], NONE)
    total_edges = jnp.sum(counts[:, 0:1])
    edge_check = jnp.where(total_edges > EDGES, FULL, edge_check)
    within = iota((128, 128), 0).astype(F32)
    edge_var = looked[1:2, :] + jnp.sum(lane_hot * within, axis=0, keepdims=True)
    weight_at = exact_dot(weights, row_hot, ((0,), (0,)))
    edge_weight = jnp.sum(weight_at * lane_hot, axis=0, keepdims=True)

    pl.semaphore_wait(barrier, 22)
    for turn in of_column:
        pl.semaphore_signal(
            entered,
            1,
            device_id={"chk": lax.bitwise_xor(i, turn // 16)},
            device_id_type=MESH_ID,
        )

    def turned(values):
        flipped = jnp.transpose(values)[0:64, :]
        odd = (iota((64, 128), 1) & 1) == 1
        return jnp.concatenate(
            [jnp.where(odd, 0.0, flipped), jnp.where(odd, flipped, 0.0)], axis=0
        )

    marks_turned = turned(marks)
    col_hot, down_hot, unused_place, unused_counts = edge_list(
        marks_turned, unique(variable_of(0)), unique(variable_of(1))
    )
    place_at = small_dot(marks_turned * turned(place), col_hot, ((0,), (0,)))
    order = jnp.sum(place_at * down_hot, axis=0, keepdims=True)

    pl.semaphore_wait(entered, 7)

    own_cell = j * 8 + i
    shot = i * 16 + j
    for kind, row in enumerate((edge_weight, edge_check, edge_var, order)):
        cell_out[:, pl.ds(kind * 128, 128)] = row
    loads[4].wait()
    for half in range(2):
        lanes = pl.ds(half * 128, 128)
        prior_out[:, lanes] = prior_ref[lanes].reshape(1, 128)
    for turn in of_row:
        send(1, prior_out, prior_in, j, turn)
    for turn in everyone:
        send(0, cell_out, cell_in, own_cell, turn)
    cell_in[pl.ds(own_cell, 1), :] = cell_out[...]
    prior_in[pl.ds(j, 1), :] = prior_out[...]
    loads[6].wait()
    signs = 1.0 - 2.0 * syndrome_ref[...].astype(F32)
    for half in range(2):
        rows = pl.ds(half * 128, 128)
        flip_ref[rows, :] = jnp.transpose(signs[half * 128 : half * 128 + 128, :])
        sigma_out[:, rows] = flip_ref[pl.ds(half * 128 + j, 8, stride=16), :]
    for turn in of_column:
        other = lax.bitwise_xor(i, turn // 16)
        send(2, sigma_out.at[pl.ds(other, 1)], sigma_in, i, turn)
    sigma_in[pl.ds(i, 1), :] = sigma_out[pl.ds(i, 1), :]
    loads[5].wait()
    for half in range(2):
        rows = pl.ds(half * 128, 128)
        flip_ref[rows, :] = jnp.transpose(cot_ref[rows, :])
        start = pl.multiple_of(half * 128 + i * 16, 16)
        cot_out[:, rows] = flip_ref[pl.ds(start, 16), :]
    for turn in of_row:
        other = lax.bitwise_xor(j, turn)
        send(3, cot_out.at[pl.ds(other, 1)], cot_in, j, turn)
    cot_in[pl.ds(j, 1), :] = cot_out[pl.ds(j, 1), :]

    def column_rows(ref):
        return tuple(
            ref[:, half * 128 : half * 128 + 128].reshape(16, 1, 128) for half in range(2)
        )

    wait_for(recv_sem, 1, prior_in, 15)
    wait_for(recv_sem, 2, sigma_in, 7)
    wait_for(recv_sem, 3, cot_in, 15)
    prior = column_rows(prior_in)
    cot = column_rows(cot_in)
    sigma = [
        jnp.concatenate([sigma_in[:, half * 128 : half * 128 + 128]] * 16, axis=0)
        for half in range(2)
    ]
    wait_for(recv_sem, 0, cell_in, 127)

    weight = cell_in[:, 0:128]
    check = cell_in[:, 128:256]
    variable = cell_in[:, 256:384].astype(jnp.int32)
    order = cell_in[:, 384:512].astype(jnp.int32)
    valid = check < 256.0
    check_index = jnp.minimum(check, 255.0).astype(jnp.int32)
    check_upper = check_index >= 128
    check_index = check_index & 127
    var_upper = variable >= 128
    var_index = variable & 127
    by_var = jnp.where(valid, take(variable.astype(F32), order), NONE)
    bad = (
        (check > 500.0)
        | (valid & (check == back(check, CHECK_SPAN)))
        | (valid & (by_var == back(by_var, VAR_SPAN)))
    )
    flag_ref[0, 0] = jnp.max(bad.astype(F32))
    same_back = {step: check == back(check, step) for step in (1, 2, 4, 7)}
    same_fore = {step: check == fore(check, step) for step in (1, 2, 4, 7)}
    same_var = {step: by_var == back(by_var, step) for step in NEAR + VAR_FAR}
    orders = {step: back(order, step) for step in NEAR}
    check_last = last_places(check)
    var_last = last_places(by_var)
    sign = pick(sigma, check_index, check_upper)

    def to_edges(rows):
        return pick([spread_rows(rows[0]), spread_rows(rows[1])], var_index, var_upper)

    def to_variables(values):
        group = take(values, order)
        for step in NEAR:
            group = group + jnp.where(same_var[step], take(values, orders[step]), 0.0)
        values = group
        for step in VAR_FAR:
            values = values + jnp.where(same_var[step], back(group, step), 0.0)
        return [
            jnp.sum(
                jnp.where(found, take(values, place), 0.0).reshape(16, 8, 128),
                axis=1,
                keepdims=True,
            )
            for place, found in var_last
        ]

    def exchange(messages):
        halves = jnp.where(valid, jnp.tanh(0.5 * messages), 1.0)
        before, saved_back = scan_products(halves, same_back, back)
        after, saved_fore = scan_products(halves, same_fore, fore)
        ahead = halves * before
        others, saved_cross = [], []
        for place, found in check_last:
            other, kept = cross_products(jnp.where(found, take(ahead, place), 1.0))
            others.append(other)
            saved_cross.append(kept)
        outside = pick(others, check_index, check_upper)
        inner = before * after
        damped = (DAMP * sign) * (inner * outside)
        level = jnp.log((1.0 + damped) / (1.0 - damped))
        saved = (halves, before, after, inner, outside, damped, saved_back, saved_fore, saved_cross)
        return level, saved

    def exchange_grad(grad_update, saved):
        halves, before, after, inner, outside, damped, saved_back, saved_fore, saved_cross = saved
        leaf = grad_update * weight * sign * ((2.0 * DAMP) / (1.0 - damped * damped))
        before_sum = scan_sums(leaf, saved_back, same_back, back)
        after_sum = scan_sums(leaf, saved_fore, same_fore, fore)
        whole = leaf * before + halves * before_sum
        outer = [
            cross_sums(jnp.where(found, take(whole, place), 0.0), kept)
            for (place, found), kept in zip(check_last, saved_cross)
        ]
        outside_sum = pick(outer, check_index, check_upper)
        grad = (before_sum * after + before * after_sum) * outside + inner * outside_sum
        return grad * (0.5 * (1.0 - halves * halves))

    level_one, saved_one = exchange(to_edges(prior))
    update = weight * level_one
    total = [a + b for a, b in zip(prior, to_variables(update))]
    level_two, saved_two = exchange(to_edges(total) - update)
    marginal = [a + b for a, b in zip(prior, to_variables(weight * level_two))]
    for half in range(2):
        for t in range(16):
            marg_out[pl.ds(t, 1), pl.ds(half * 128, 128)] = marginal[half][t]
    for turn in everyone:
        other = lax.bitwise_xor(j, turn % 16)
        send(4, marg_out.at[pl.ds(other, 1)], marg_in, shot, turn)
    marg_in[pl.ds(shot, 1), :] = marg_out[pl.ds(j, 1), :]
    edge_cot = to_edges(cot)
    grad_message = exchange_grad(edge_cot, saved_two)
    grad_total = to_variables(grad_message)
    grad_update = to_edges(grad_total) - grad_message
    grad_weight = edge_cot * level_two + grad_update * level_one
    weight_out[...] = grad_weight
    for turn in everyone:
        other = lax.bitwise_xor(j, turn % 16) * 8 + lax.bitwise_xor(i, turn // 16)
        send(5, weight_out.at[pl.ds(other, 1)], weight_in, shot, turn)
    weight_in[pl.ds(shot, 1), :] = weight_out[pl.ds(own_cell, 1), :]

    grad_first = to_variables(exchange_grad(grad_update, saved_one))
    for half in range(2):
        grad_prior = cot[half] + grad_total[half] + grad_first[half]
        for t in range(16):
            late_out[pl.ds(t, 1), pl.ds(half * 128, 128)] = grad_prior[t]
    for turn in everyone:
        other = lax.bitwise_xor(j, turn % 16)
        send(6, late_out.at[pl.ds(other, 1)], late_in, shot, turn)
    late_in[pl.ds(shot, 1), :] = late_out[pl.ds(j, 1), :]

    wait_for(recv_sem, 4, marg_in, 127)
    for half in range(2):
        marg_ref[pl.ds(half * 128, 128), :] = jnp.transpose(
            marg_in[:, half * 128 : half * 128 + 128]
        )
    wait_for(recv_sem, 5, weight_in, 127)
    edge_grad = jnp.sum(weight_in[...], axis=0, keepdims=True)
    spread = row_hot_ref[...] * edge_grad
    hot = lane_hot_ref[0:64, :]
    nothing = jnp.zeros((64, 128), F32)
    dense = exact_dot(
        spread[0:64, :], jnp.concatenate([hot, nothing], axis=0), ((1,), (1,))
    ) + exact_dot(spread[64:128, :], jnp.concatenate([nothing, hot], axis=0), ((1,), (1,)))
    for m in range(32):
        wgrad_ref[0, 0, :, pl.ds(m * 128, 128)] = dense[m * 2 : m * 2 + 2, :]
    wait_for(recv_sem, 6, late_in, 127)
    for half in range(2):
        lanes = pl.ds(half * 128, 128)
        pgrad_ref[lanes] = jnp.sum(late_in[:, half * 128 : half * 128 + 128], axis=0)

    wait_for(send_sem, 0, cell_in, 127)
    wait_for(send_sem, 1, prior_in, 15)
    wait_for(send_sem, 2, sigma_in, 7)
    wait_for(send_sem, 3, cot_in, 15)
    wait_for(send_sem, 4, marg_in, 127)
    wait_for(send_sem, 5, weight_in, 127)
    wait_for(send_sem, 6, late_in, 127)


def finish_kernel(marg_in, wgrad_in, pgrad_in, marg_out, wgrad_out, pgrad_out, sems):
    copies = [
        pltpu.make_async_copy(given, out, sems.at[at])
        for at, (given, out) in enumerate(
            ((marg_in, marg_out), (wgrad_in, wgrad_out), (pgrad_in, pgrad_out))
        )
    ]
    for copy in copies:
        copy.start()
    for copy in copies:
        copy.wait()


VMEM_SPEC = pl.BlockSpec(memory_space=pltpu.VMEM)
SMEM_SPEC = pl.BlockSpec(memory_space=pltpu.SMEM)
ANY_SPEC = pl.BlockSpec(memory_space=pl.ANY)


def sparse_parts(tile_bits, tile_pos, tile_count, edge_weight, syndrome, channel_prior, out_cot):
    shape = jax.ShapeDtypeStruct
    held = [
        pltpu.SMEM(tile_count.shape, jnp.int32),
        pltpu.SMEM(tile_pos.shape, jnp.int32),
        pltpu.VMEM(tile_bits.shape, jnp.int32),
        pltpu.VMEM(edge_weight.shape, F32),
        pltpu.VMEM(syndrome.shape, jnp.int32),
        pltpu.VMEM(channel_prior.shape, F32),
        pltpu.VMEM(out_cot.shape, F32),
        pltpu.SemaphoreType.DMA((7,)),
    ]
    work = [(64, 128), (64, 128), (128, 128), (128, 128), (256, 128)]
    exchanged = [
        (1, 512), (128, 512), (1, 256), (16, 256), (8, 256), (8, 256), (16, 256), (16, 256),
        (16, 256), (128, 256), (128, 128), (128, 128), (16, 256), (128, 256),
    ]
    return pl.pallas_call(
        sparse_kernel,
        out_shape=(
            shape(out_cot.shape, F32),
            shape(edge_weight.shape, F32),
            shape(channel_prior.shape, F32),
            shape((1, 1), F32),
        ),
        in_specs=[ANY_SPEC] * 7,
        out_specs=(VMEM_SPEC,) * 3 + (SMEM_SPEC,),
        scratch_shapes=held
        + [pltpu.VMEM(extent, F32) for extent in work + exchanged]
        + [pltpu.VMEM((127, tiles, 128), F32) for tiles in (1, 2, 4)]
        + [
            pltpu.SemaphoreType.REGULAR,
            pltpu.SemaphoreType.DMA((7,)),
            pltpu.SemaphoreType.DMA((7,)),
        ],
        compiler_params=pltpu.CompilerParams(
            collective_id=0, has_side_effects=True, vmem_limit_bytes=48 << 20
        ),
    )(tile_count, tile_pos, tile_bits, edge_weight, syndrome, channel_prior, out_cot)


def finish(*parts):
    return pl.pallas_call(
        finish_kernel,
        out_shape=tuple(jax.ShapeDtypeStruct(part.shape, part.dtype) for part in parts),
        in_specs=[ANY_SPEC] * 3,
        out_specs=(ANY_SPEC,) * 3,
        scratch_shapes=[pltpu.SemaphoreType.DMA((3,))],
    )(*parts)


def body(*arguments):
    *parts, flag = sparse_parts(*arguments)
    return lax.cond(
        flag[0, 0] > 0.0,
        lambda given, kept: dense_body(*given),
        lambda given, kept: tuple(finish(*kept)),
        arguments,
        tuple(parts),
    )


def solution(mesh):
    placed = (
        P("chk", "var", None, None),
        P("chk", "var", None, None),
        P("chk", "var"),
        P("chk", "var", None, None),
        P("chk", None),
        P("var"),
        P("var", None),
    )
    return jax.shard_map(
        body,
        mesh=mesh,
        in_specs=placed,
        out_specs=(P("var", None), P("chk", "var", None, None), P("var")),
        check_vma=False,
    )
```

```python
import jax
import jax.numpy as jnp
from jax import lax
from jax.experimental import pallas as pl
from jax.experimental.pallas import tpu as pltpu
from jax.sharding import PartitionSpec as P

TILE = 64
ITERS = 2


DAMP = 0.97
EXACT = lax.Precision.HIGHEST


def linear_both(values, axis):
    length = values.shape[axis]
    pieces = [lax.slice_in_dim(values, index, index + 1, axis=axis) for index in range(length)]
    ones = jnp.ones_like(pieces[0])
    prefix = [ones]
    for index in range(length - 1):
        prefix.append(prefix[-1] * pieces[index])
    suffix = [ones]
    for index in range(length - 1, 0, -1):
        suffix.append(suffix[-1] * pieces[index])
    suffix = suffix[::-1]
    whole = prefix[-1] * pieces[-1]
    return (jnp.concatenate(prefix, axis=axis), jnp.concatenate(suffix, axis=axis), whole)


def exclusive_both(values, axis):
    length = values.shape[axis]
    if length < 16 or length % 8 != 0:
        return linear_both(values, axis)
    shape = values.shape
    split = values.reshape(shape[:axis] + (length // 8, 8) + shape[axis + 1 :])
    inner_before, inner_after, group_whole = linear_both(split, axis + 1)
    outer_before, outer_after, whole = exclusive_both(group_whole, axis)
    before = (inner_before * outer_before).reshape(shape)
    after = (inner_after * outer_after).reshape(shape)
    whole = whole.reshape(shape[:axis] + (1,) + shape[axis + 1 :])
    return (before, after, whole)


def device_tables(bits, positions, count, check_blocks, column_blocks):
    slot_total = bits.shape[0]
    slots = jnp.arange(slot_total, dtype=jnp.int32)
    live = slots < count
    edge = jnp.where(live[:, None], bits, 0).astype(jnp.float32).reshape(slot_total, TILE, TILE)
    row_hot = (positions[:, 0:1] == jnp.arange(check_blocks, dtype=jnp.int32)[None, :]).astype(
        jnp.float32
    )
    col_hot = (positions[:, 1:2] == jnp.arange(column_blocks, dtype=jnp.int32)[None, :]).astype(
        jnp.float32
    )
    same_row = (positions[:, None, 0] == positions[None, :, 0]) & (slots[:, None] != slots[None, :])
    return (edge, row_hot, col_hot, same_row)


def row_products(messages, edge, row_hot, same_row):
    halves = jnp.where(edge[..., None] > 0, jnp.tanh(0.5 * messages), 1.0)
    before, after, whole = exclusive_both(halves, 2)
    whole = whole[:, :, 0, :]
    rows = jnp.prod(jnp.where(row_hot[:, :, None, None] > 0, whole[:, None], 1.0), axis=0)
    others_here = jnp.prod(jnp.where(same_row[:, :, None, None], whole[None], 1.0), axis=1)
    inner = before * after * others_here[:, :, None, :]
    return (inner, rows)


def edge_messages(inner, others, weight, sign_slot, edge, row_hot, col_hot):
    others_slot = jnp.einsum("kc,crs->krs", row_hot, others, precision=EXACT)
    product = sign_slot[:, :, None, :] * inner * others_slot[:, :, None, :]
    update = (edge * weight)[..., None] * jnp.log((1.0 + DAMP * product) / (1.0 - DAMP * product))
    column = jnp.einsum("kv,kcs->vcs", col_hot, jnp.sum(update, axis=1), precision=EXACT)
    return (update, column)


def column_sum(values, col_hot):
    return jnp.einsum("kv,kcs->vcs", col_hot, jnp.sum(values, axis=1), precision=EXACT)


def gather_all(values, axis):
    shape = values.shape
    rows = values.size // shape[-1]
    size = lax.axis_size(axis)

    def kernel(given, out, send_sem, recv_sem):
        me = lax.axis_index(axis)
        barrier = pltpu.get_barrier_semaphore()
        for step in range(1, size):
            pl.semaphore_signal(
                barrier,
                1,
                device_id={axis: lax.rem(me + step, size)},
                device_id_type=pl.DeviceIdType.MESH,
            )
        pl.semaphore_wait(barrier, size - 1)
        own = out.at[me]
        for step in range(1, size):
            pltpu.make_async_remote_copy(
                src_ref=given,
                dst_ref=own,
                send_sem=send_sem,
                recv_sem=recv_sem,
                device_id={axis: lax.rem(me + step, size)},
                device_id_type=pl.DeviceIdType.MESH,
            ).start()
        own[...] = given[...]
        whole = out.at[pl.ds(0, size - 1)]
        pltpu.make_async_copy(whole, whole, recv_sem).wait()
        pltpu.make_async_copy(whole, whole, send_sem).wait()

    gathered = pl.pallas_call(
        kernel,
        out_shape=jax.ShapeDtypeStruct((size, rows, shape[-1]), values.dtype),
        in_specs=[pl.BlockSpec(memory_space=pltpu.VMEM)],
        out_specs=pl.BlockSpec(memory_space=pltpu.VMEM),
        scratch_shapes=[pltpu.SemaphoreType.DMA, pltpu.SemaphoreType.DMA],
        compiler_params=pltpu.CompilerParams(
            collective_id=1 if axis == "chk" else 2, has_side_effects=True
        ),
    )(values.reshape(rows, shape[-1]))
    return gathered.reshape((size,) + shape)


def gather_blocks(values):
    return gather_all(values, "var").reshape((-1,) + values.shape[1:])


def checks_total(values):
    return jnp.sum(gather_all(values, "chk"), axis=0)


def others_forward(rows, check_blocks):
    own = lax.axis_index("var")
    carry = jnp.ones_like(rows)
    piece = gather_blocks(rows)
    indices = jnp.arange(piece.shape[0], dtype=jnp.int32)
    keep = indices // check_blocks != own
    parts = []
    for block in range(check_blocks):
        pick = (keep & (indices % check_blocks == block))[:, None, None]
        parts.append(carry[block] * jnp.prod(jnp.where(pick, piece, 1.0), axis=0))
    others = jnp.stack(parts)
    return (others, (rows, rows))


def others_backward(rows, grads, check_blocks):
    own = lax.axis_index("var")
    kept_products = jnp.ones_like(rows)
    kept_sums = jnp.zeros_like(rows)
    row_piece = gather_blocks(rows)
    grad_piece = gather_blocks(grads)
    indices = jnp.arange(row_piece.shape[0], dtype=jnp.int32)
    keep = indices // check_blocks != own
    new_products = []
    new_sums = []
    for block in range(check_blocks):
        pick = (keep & (indices % check_blocks == block))[:, None, None]
        factors = jnp.where(pick, row_piece, 1.0)
        weights = jnp.where(pick, grad_piece, 0.0)
        before, after, whole = exclusive_both(factors, 0)
        within = jnp.sum(weights * before * after, axis=0)
        whole = whole[0]
        new_sums.append(kept_sums[block] * whole + kept_products[block] * within)
        new_products.append(kept_products[block] * whole)
    return jnp.stack(new_sums)


def dense_body(tile_bits, tile_pos, tile_count, edge_weight, syndrome, channel_prior, out_cot):
    slot_total = tile_bits.shape[2]
    shots = syndrome.shape[1]
    check_blocks = syndrome.shape[0] // TILE
    column_blocks = channel_prior.shape[0] // TILE
    edge, row_hot, col_hot, same_row = device_tables(
        tile_bits[0, 0], tile_pos[0, 0], tile_count[0, 0], check_blocks, column_blocks
    )
    weight = edge_weight[0, 0].reshape(slot_total, TILE, TILE)
    sign_dev = (1.0 - 2.0 * syndrome.astype(jnp.float32)).reshape(check_blocks, TILE, shots)
    sign_slot = jnp.einsum("kc,crs->krs", row_hot, sign_dev, precision=EXACT)
    prior_dev = channel_prior.reshape(column_blocks, TILE)
    prior_slot = jnp.einsum("kv,vc->kc", col_hot, prior_dev, precision=EXACT)
    messages = jnp.broadcast_to(prior_slot[:, None, :, None], (slot_total, TILE, TILE, shots))
    saved = []
    total = None
    for step in range(ITERS):
        inner, rows = row_products(messages, edge, row_hot, same_row)
        others, kept = others_forward(rows, check_blocks)
        update, column = edge_messages(inner, others, weight, sign_slot, edge, row_hot, col_hot)
        total = prior_dev[:, :, None] + checks_total(column)
        saved.append((messages, inner, rows, others, kept))
        if step + 1 < ITERS:
            spread = jnp.einsum("kv,vcs->kcs", col_hot, total, precision=EXACT)
            messages = spread[:, None] - update
    marginals = total.reshape(column_blocks * TILE, shots)
    grad_total = out_cot.reshape(column_blocks, TILE, shots)
    grad_update = jnp.zeros((slot_total, TILE, TILE, shots), jnp.float32)
    prior_grad = jnp.zeros((column_blocks, TILE), jnp.float32)
    weight_grad = jnp.zeros_like(weight)
    for step in reversed(range(ITERS)):
        messages_now, inner, rows, others, kept = saved[step]
        prior_grad = prior_grad + jnp.sum(grad_total, axis=2)

        def message_part(inner_now, others_now, weight_now):
            return edge_messages(
                inner_now, others_now, weight_now, sign_slot, edge, row_hot, col_hot
            )

        unused, pull = jax.vjp(message_part, inner, others, weight)
        grad_inner, grad_others, weight_part = pull((grad_update, grad_total))
        weight_grad = weight_grad + weight_part
        grad_rows = others_backward(rows, grad_others, check_blocks)

        def product_part(messages_in):
            return row_products(messages_in, edge, row_hot, same_row)

        unused_rows, pull_rows = jax.vjp(product_part, messages_now)
        grad_messages = pull_rows((grad_inner, grad_rows))[0]
        grad_total = checks_total(column_sum(grad_messages, col_hot))
        grad_update = -grad_messages
    prior_grad = prior_grad + jnp.sum(grad_total, axis=2)
    return (
        marginals,
        weight_grad.reshape(1, 1, slot_total, TILE * TILE),
        prior_grad.reshape(column_blocks * TILE),
    )


EDGES = 128
NEAR = (1, 2)
FAR = (1, 4, 7)
VAR_FAR = (3, 6, 9)
CHECK_SPAN = 10
VAR_SPAN = 12
NONE = 300.0
FULL = 1000.0
MESH_ID = pl.DeviceIdType.MESH
F32 = jnp.float32
BF16 = jnp.bfloat16


def iota(shape, axis):
    return lax.broadcasted_iota(jnp.int32, shape, axis)


def take(values, index):
    return jnp.take_along_axis(values, index, axis=1, mode="promise_in_bounds")


def small_dot(left, right, dims):
    return lax.dot_general(
        left.astype(BF16), right.astype(BF16), (dims, ((), ())), preferred_element_type=F32
    )


def exact_dot(left, right, dims):
    return lax.dot_general(
        left, right, (dims, ((), ())), precision=EXACT, preferred_element_type=F32
    )


def edge_list(marks, key_rows, key_lanes):
    ahead = (iota((128, 128), 0) < iota((128, 128), 1)).astype(F32)
    within = small_dot(marks, ahead, ((1,), (0,)))
    counts = small_dot(marks, jnp.ones((128, 128), F32), ((1,), (0,)))
    lower = (key_lanes < key_rows).astype(F32)
    start = small_dot(lower, counts, ((1,), (0,)))
    place = iota((128, 128), 1).astype(F32)
    row_hot = ((place >= start) & (place < start + counts)).astype(F32)
    wanted = jnp.sum(row_hot * (place - start + 1.0), axis=0, keepdims=True)
    ranks = small_dot(marks * (within + 1.0), row_hot, ((0,), (0,)))
    lane_hot = ((ranks == wanted) & (wanted > 0.0)).astype(F32)
    return row_hot, lane_hot, start + within, counts


def cells(values):
    return [values[j * 8 : j * 8 + 8, :] for j in range(16)]


def spread_rows(rows):
    return jnp.broadcast_to(rows, (16, 8, 128)).reshape(128, 128)


def pick(pair, index, upper):
    return jnp.where(upper, take(pair[1], index), take(pair[0], index))


def last_places(order):
    out = []
    marks = [
        jnp.broadcast_to(order[:, at : at + 1], (128, 128)) for at in range(15, 128, 16)
    ]
    for half in range(2):
        key = (iota((128, 128), 1) + 128 * half).astype(F32)
        place = jnp.zeros((128, 128), jnp.int32)
        seen = jnp.full((128, 128), -1.0, F32)
        for mark in marks:
            fits = mark <= key
            place = jnp.where(fits, place + 16, place)
            seen = jnp.where(fits, mark, seen)
        for step in (8, 4, 2, 1):
            value = take(order, jnp.minimum(place + (step - 1), 127))
            fits = value <= key
            place = jnp.where(fits, place + step, place)
            seen = jnp.where(fits, value, seen)
        out.append((jnp.clip(place - 1, 0, 127), seen == key))
    return out


def back(values, step):
    return pltpu.roll(values, step, 1)


def fore(values, step):
    return pltpu.roll(values, 128 - step, 1)


def scan_products(values, same, shift):
    one, two = (jnp.where(same[step], shift(values, step), 1.0) for step in NEAR)
    group = values * one * two
    far = [jnp.where(same[step], shift(group, step), 1.0) for step in FAR]
    return far[0] * far[1] * far[2], (values, one, two, far)


def scan_sums(sums, saved, same, shift):
    values, one, two, far = saved
    one_sum, two_sum = (jnp.where(same[step], shift(sums, step), 0.0) for step in NEAR)
    group = (sums * one + values * one_sum) * two + (values * one) * two_sum
    a, b, c = (jnp.where(same[step], shift(group, step), 0.0) for step in FAR)
    return (a * far[1] + far[0] * b) * far[2] + (far[0] * far[1]) * c


def cross_products(rows):
    pieces = cells(rows)
    first = [jnp.ones((8, 128), F32)]
    for j in range(15):
        first.append(first[-1] * pieces[j])
    last = [jnp.ones((8, 128), F32)]
    for j in range(15, 0, -1):
        last.append(last[-1] * pieces[j])
    last = last[::-1]
    others = jnp.concatenate([a * b for a, b in zip(first, last)], axis=0)
    return others, (pieces, first, last)


def cross_sums(rows, saved):
    pieces, first, last = saved
    sums = cells(rows)
    first_sum = [jnp.zeros((8, 128), F32)]
    for j in range(15):
        first_sum.append(first_sum[-1] * pieces[j] + first[j] * sums[j])
    last_sum = [jnp.zeros((8, 128), F32)]
    for j in range(15, 0, -1):
        last_sum.append(last_sum[-1] * pieces[j] + last[j] * sums[j])
    last_sum = last_sum[::-1]
    return jnp.concatenate(
        [first_sum[j] * last[j] + first[j] * last_sum[j] for j in range(16)], axis=0
    )


def sparse_kernel(
    count_hbm, pos_hbm, bits_hbm, weight_hbm, syndrome_hbm, prior_hbm, cot_hbm,
    marg_ref, wgrad_ref, pgrad_ref, flag_ref,
    count_ref, pos_ref, bits_ref, weight_ref, syndrome_ref, prior_ref, cot_ref, load_sem,
    raw_bits, raw_weight, row_hot_ref, lane_hot_ref, flip_ref,
    cell_out, cell_in, prior_out, prior_in, sigma_out, sigma_in, cot_out, cot_in,
    marg_out, marg_in, weight_out, weight_in, late_out, late_in,
    size_1, size_2, size_4, send_sem, recv_sem,
):
    row_sizes = {1: size_1, 2: size_2, 4: size_4}
    i = lax.axis_index("chk")
    j = lax.axis_index("var")
    barrier = pltpu.get_barrier_semaphore()
    loads = [
        pltpu.make_async_copy(given, held, load_sem.at[at])
        for at, (given, held) in enumerate(
            (
                (count_hbm, count_ref),
                (pos_hbm, pos_ref),
                (bits_hbm, bits_ref),
                (weight_hbm, weight_ref),
                (prior_hbm, prior_ref),
                (cot_hbm, cot_ref),
                (syndrome_hbm, syndrome_ref),
            )
        )
    ]
    for load in loads:
        load.start()
    everyone = sorted(range(1, 128), key=lambda turn: -bin(turn).count("1"))
    of_row = [turn for turn in everyone if turn < 16]
    of_column = [turn for turn in everyone if turn % 16 == 0]

    def device(turn):
        return {
            "chk": lax.bitwise_xor(i, turn // 16),
            "var": lax.bitwise_xor(j, turn % 16),
        }

    for turn in everyone:
        pl.semaphore_signal(barrier, 1, device_id=device(turn), device_id_type=MESH_ID)

    def send(phase, source, target, row, turn):
        pltpu.make_async_remote_copy(
            src_ref=source,
            dst_ref=target.at[pl.ds(row, 1)],
            send_sem=send_sem.at[phase],
            recv_sem=recv_sem.at[phase],
            device_id=device(turn),
            device_id_type=MESH_ID,
        ).start()

    def wait_for(sems, phase, target, count):
        whole = row_sizes[target.shape[1] // 128].at[pl.ds(0, count)]
        pltpu.make_async_copy(whole, whole, sems.at[phase]).wait()

    for load in loads[0:4]:
        load.wait()
    count = count_ref[0, 0]
    live = (iota((2, 128), 0) < count).astype(F32)
    for m in range(32):
        lanes = pl.ds(m * 128, 128)
        raw_bits[pl.ds(m * 2, 2), :] = bits_ref[0, 0, :, lanes].astype(F32) * live
        raw_weight[pl.ds(m * 2, 2), :] = weight_ref[0, 0, :, lanes]
    narrow = iota((64, 128), 1) < 64

    def entries(ref):
        value = ref[...]
        low = jnp.where(narrow, value, 0.0)
        high = jnp.where(narrow, pltpu.roll(value, 64, 1), 0.0)
        return jnp.concatenate([low, high], axis=0)

    marks = entries(raw_bits)
    weights = entries(raw_weight)
    p0, p1 = pos_ref[0, 0, 0, 0], pos_ref[0, 0, 1, 0]
    q0, q1 = pos_ref[0, 0, 0, 1], pos_ref[0, 0, 1, 1]

    def check_of(axis, shape=(128, 128)):
        at = iota(shape, axis)
        slot = at & 1
        return jnp.where(slot == 0, p0, p1) * 64 + (at & 62) + (at >> 6), slot

    def variable_of(axis):
        at = iota((128, 128), axis)
        slot = at >> 6
        return jnp.where(slot == 0, q0, q1) * 64 + (at & 63), slot

    def unique(pair):
        return pair[0] * 2 + pair[1]

    row_hot, lane_hot, place, counts = edge_list(
        marks, unique(check_of(0)), unique(check_of(1))
    )
    row_hot_ref[...] = row_hot
    lane_hot_ref[...] = lane_hot
    checks, slots = check_of(1, (8, 128))
    columns = jnp.where(slots == 0, q0, q1) * 64
    table = jnp.where(
        iota((8, 128), 0) == 0,
        checks,
        jnp.where(iota((8, 128), 0) == 1, columns, 1),
    ).astype(F32)
    looked = small_dot(table, row_hot, ((1,), (0,)))
    present = looked[2:3, :] > 0.0
    edge_check = jnp.where(present, looked[0:1, :], NONE)
    total_edges = jnp.sum(counts[:, 0:1])
    edge_check = jnp.where(total_edges > EDGES, FULL, edge_check)
    within = iota((128, 128), 0).astype(F32)
    edge_var = looked[1:2, :] + jnp.sum(lane_hot * within, axis=0, keepdims=True)
    weight_at = exact_dot(weights, row_hot, ((0,), (0,)))
    edge_weight = jnp.sum(weight_at * lane_hot, axis=0, keepdims=True)

    def turned(values):
        flipped = jnp.transpose(values)[0:64, :]
        odd = (iota((64, 128), 1) & 1) == 1
        return jnp.concatenate(
            [jnp.where(odd, 0.0, flipped), jnp.where(odd, flipped, 0.0)], axis=0
        )

    marks_turned = turned(marks)
    col_hot, down_hot, unused_place, unused_counts = edge_list(
        marks_turned, unique(variable_of(0)), unique(variable_of(1))
    )
    place_at = small_dot(marks_turned * turned(place), col_hot, ((0,), (0,)))
    order = jnp.sum(place_at * down_hot, axis=0, keepdims=True)

    pl.semaphore_wait(barrier, 127)

    own_cell = j * 8 + i
    shot = i * 16 + j
    for kind, row in enumerate((edge_weight, edge_check, edge_var, order)):
        cell_out[:, pl.ds(kind * 128, 128)] = row
    loads[4].wait()
    for half in range(2):
        lanes = pl.ds(half * 128, 128)
        prior_out[:, lanes] = prior_ref[lanes].reshape(1, 128)
    for turn in of_row:
        send(1, prior_out, prior_in, j, turn)
    for turn in everyone:
        send(0, cell_out, cell_in, own_cell, turn)
    cell_in[pl.ds(own_cell, 1), :] = cell_out[...]
    prior_in[pl.ds(j, 1), :] = prior_out[...]
    loads[6].wait()
    signs = 1.0 - 2.0 * syndrome_ref[...].astype(F32)
    for half in range(2):
        rows = pl.ds(half * 128, 128)
        flip_ref[rows, :] = jnp.transpose(signs[half * 128 : half * 128 + 128, :])
        sigma_out[:, rows] = flip_ref[pl.ds(half * 128 + j, 8, stride=16), :]
    for turn in of_column:
        other = lax.bitwise_xor(i, turn // 16)
        send(2, sigma_out.at[pl.ds(other, 1)], sigma_in, i, turn)
    sigma_in[pl.ds(i, 1), :] = sigma_out[pl.ds(i, 1), :]
    loads[5].wait()
    for half in range(2):
        rows = pl.ds(half * 128, 128)
        flip_ref[rows, :] = jnp.transpose(cot_ref[rows, :])
        start = pl.multiple_of(half * 128 + i * 16, 16)
        cot_out[:, rows] = flip_ref[pl.ds(start, 16), :]
    for turn in of_row:
        other = lax.bitwise_xor(j, turn)
        send(3, cot_out.at[pl.ds(other, 1)], cot_in, j, turn)
    cot_in[pl.ds(j, 1), :] = cot_out[pl.ds(j, 1), :]

    def column_rows(ref):
        return tuple(
            ref[:, half * 128 : half * 128 + 128].reshape(16, 1, 128) for half in range(2)
        )

    wait_for(recv_sem, 1, prior_in, 15)
    wait_for(recv_sem, 2, sigma_in, 7)
    wait_for(recv_sem, 3, cot_in, 15)
    prior = column_rows(prior_in)
    cot = column_rows(cot_in)
    sigma = [
        jnp.concatenate([sigma_in[:, half * 128 : half * 128 + 128]] * 16, axis=0)
        for half in range(2)
    ]
    wait_for(recv_sem, 0, cell_in, 127)

    weight = cell_in[:, 0:128]
    check = cell_in[:, 128:256]
    variable = cell_in[:, 256:384].astype(jnp.int32)
    order = cell_in[:, 384:512].astype(jnp.int32)
    valid = check < 256.0
    check_index = jnp.minimum(check, 255.0).astype(jnp.int32)
    check_upper = check_index >= 128
    check_index = check_index & 127
    var_upper = variable >= 128
    var_index = variable & 127
    by_var = jnp.where(valid, take(variable.astype(F32), order), NONE)
    bad = (
        (check > 500.0)
        | (valid & (check == back(check, CHECK_SPAN)))
        | (valid & (by_var == back(by_var, VAR_SPAN)))
    )
    flag_ref[0, 0] = jnp.max(bad.astype(F32))
    same_back = {step: check == back(check, step) for step in (1, 2, 4, 7)}
    same_fore = {step: check == fore(check, step) for step in (1, 2, 4, 7)}
    same_var = {step: by_var == back(by_var, step) for step in NEAR + VAR_FAR}
    orders = {step: back(order, step) for step in NEAR}
    check_last = last_places(check)
    var_last = last_places(by_var)
    sign = pick(sigma, check_index, check_upper)

    def to_edges(rows):
        return pick([spread_rows(rows[0]), spread_rows(rows[1])], var_index, var_upper)

    def to_variables(values):
        group = take(values, order)
        for step in NEAR:
            group = group + jnp.where(same_var[step], take(values, orders[step]), 0.0)
        values = group
        for step in VAR_FAR:
            values = values + jnp.where(same_var[step], back(group, step), 0.0)
        return [
            jnp.sum(
                jnp.where(found, take(values, place), 0.0).reshape(16, 8, 128),
                axis=1,
                keepdims=True,
            )
            for place, found in var_last
        ]

    def exchange(messages):
        halves = jnp.where(valid, jnp.tanh(0.5 * messages), 1.0)
        before, saved_back = scan_products(halves, same_back, back)
        after, saved_fore = scan_products(halves, same_fore, fore)
        ahead = halves * before
        others, saved_cross = [], []
        for place, found in check_last:
            other, kept = cross_products(jnp.where(found, take(ahead, place), 1.0))
            others.append(other)
            saved_cross.append(kept)
        outside = pick(others, check_index, check_upper)
        inner = before * after
        damped = (DAMP * sign) * (inner * outside)
        level = jnp.log((1.0 + damped) / (1.0 - damped))
        saved = (halves, before, after, inner, outside, damped, saved_back, saved_fore, saved_cross)
        return level, saved

    def exchange_grad(grad_update, saved):
        halves, before, after, inner, outside, damped, saved_back, saved_fore, saved_cross = saved
        leaf = grad_update * weight * sign * ((2.0 * DAMP) / (1.0 - damped * damped))
        before_sum = scan_sums(leaf, saved_back, same_back, back)
        after_sum = scan_sums(leaf, saved_fore, same_fore, fore)
        whole = leaf * before + halves * before_sum
        outer = [
            cross_sums(jnp.where(found, take(whole, place), 0.0), kept)
            for (place, found), kept in zip(check_last, saved_cross)
        ]
        outside_sum = pick(outer, check_index, check_upper)
        grad = (before_sum * after + before * after_sum) * outside + inner * outside_sum
        return grad * (0.5 * (1.0 - halves * halves))

    level_one, saved_one = exchange(to_edges(prior))
    update = weight * level_one
    total = [a + b for a, b in zip(prior, to_variables(update))]
    level_two, saved_two = exchange(to_edges(total) - update)
    marginal = [a + b for a, b in zip(prior, to_variables(weight * level_two))]
    for half in range(2):
        for t in range(16):
            marg_out[pl.ds(t, 1), pl.ds(half * 128, 128)] = marginal[half][t]
    for turn in everyone:
        other = lax.bitwise_xor(j, turn % 16)
        send(4, marg_out.at[pl.ds(other, 1)], marg_in, shot, turn)
    marg_in[pl.ds(shot, 1), :] = marg_out[pl.ds(j, 1), :]
    edge_cot = to_edges(cot)
    grad_message = exchange_grad(edge_cot, saved_two)
    grad_total = to_variables(grad_message)
    grad_update = to_edges(grad_total) - grad_message
    grad_weight = edge_cot * level_two + grad_update * level_one
    weight_out[...] = grad_weight
    for turn in everyone:
        other = lax.bitwise_xor(j, turn % 16) * 8 + lax.bitwise_xor(i, turn // 16)
        send(5, weight_out.at[pl.ds(other, 1)], weight_in, shot, turn)
    weight_in[pl.ds(shot, 1), :] = weight_out[pl.ds(own_cell, 1), :]

    grad_first = to_variables(exchange_grad(grad_update, saved_one))
    for half in range(2):
        grad_prior = cot[half] + grad_total[half] + grad_first[half]
        for t in range(16):
            late_out[pl.ds(t, 1), pl.ds(half * 128, 128)] = grad_prior[t]
    for turn in everyone:
        other = lax.bitwise_xor(j, turn % 16)
        send(6, late_out.at[pl.ds(other, 1)], late_in, shot, turn)
    late_in[pl.ds(shot, 1), :] = late_out[pl.ds(j, 1), :]

    wait_for(recv_sem, 4, marg_in, 127)
    for half in range(2):
        marg_ref[pl.ds(half * 128, 128), :] = jnp.transpose(
            marg_in[:, half * 128 : half * 128 + 128]
        )
    wait_for(recv_sem, 5, weight_in, 127)
    edge_grad = jnp.sum(weight_in[...], axis=0, keepdims=True)
    spread = row_hot_ref[...] * edge_grad
    hot = lane_hot_ref[0:64, :]
    nothing = jnp.zeros((64, 128), F32)
    dense = exact_dot(
        spread[0:64, :], jnp.concatenate([hot, nothing], axis=0), ((1,), (1,))
    ) + exact_dot(spread[64:128, :], jnp.concatenate([nothing, hot], axis=0), ((1,), (1,)))
    for m in range(32):
        wgrad_ref[0, 0, :, pl.ds(m * 128, 128)] = dense[m * 2 : m * 2 + 2, :]
    wait_for(recv_sem, 6, late_in, 127)
    for half in range(2):
        lanes = pl.ds(half * 128, 128)
        pgrad_ref[lanes] = jnp.sum(late_in[:, half * 128 : half * 128 + 128], axis=0)

    wait_for(send_sem, 0, cell_in, 127)
    wait_for(send_sem, 1, prior_in, 15)
    wait_for(send_sem, 2, sigma_in, 7)
    wait_for(send_sem, 3, cot_in, 15)
    wait_for(send_sem, 4, marg_in, 127)
    wait_for(send_sem, 5, weight_in, 127)
    wait_for(send_sem, 6, late_in, 127)


def finish_kernel(marg_in, wgrad_in, pgrad_in, marg_out, wgrad_out, pgrad_out, sems):
    copies = [
        pltpu.make_async_copy(given, out, sems.at[at])
        for at, (given, out) in enumerate(
            ((marg_in, marg_out), (wgrad_in, wgrad_out), (pgrad_in, pgrad_out))
        )
    ]
    for copy in copies:
        copy.start()
    for copy in copies:
        copy.wait()


VMEM_SPEC = pl.BlockSpec(memory_space=pltpu.VMEM)
SMEM_SPEC = pl.BlockSpec(memory_space=pltpu.SMEM)
ANY_SPEC = pl.BlockSpec(memory_space=pl.ANY)


def sparse_parts(tile_bits, tile_pos, tile_count, edge_weight, syndrome, channel_prior, out_cot):
    shape = jax.ShapeDtypeStruct
    held = [
        pltpu.SMEM(tile_count.shape, jnp.int32),
        pltpu.SMEM(tile_pos.shape, jnp.int32),
        pltpu.VMEM(tile_bits.shape, jnp.int32),
        pltpu.VMEM(edge_weight.shape, F32),
        pltpu.VMEM(syndrome.shape, jnp.int32),
        pltpu.VMEM(channel_prior.shape, F32),
        pltpu.VMEM(out_cot.shape, F32),
        pltpu.SemaphoreType.DMA((7,)),
    ]
    work = [(64, 128), (64, 128), (128, 128), (128, 128), (256, 128)]
    exchanged = [
        (1, 512), (128, 512), (1, 256), (16, 256), (8, 256), (8, 256), (16, 256), (16, 256),
        (16, 256), (128, 256), (128, 128), (128, 128), (16, 256), (128, 256),
    ]
    return pl.pallas_call(
        sparse_kernel,
        out_shape=(
            shape(out_cot.shape, F32),
            shape(edge_weight.shape, F32),
            shape(channel_prior.shape, F32),
            shape((1, 1), F32),
        ),
        in_specs=[ANY_SPEC] * 7,
        out_specs=(VMEM_SPEC,) * 3 + (SMEM_SPEC,),
        scratch_shapes=held
        + [pltpu.VMEM(extent, F32) for extent in work + exchanged]
        + [pltpu.VMEM((127, tiles, 128), F32) for tiles in (1, 2, 4)]
        + [
            pltpu.SemaphoreType.DMA((7,)),
            pltpu.SemaphoreType.DMA((7,)),
        ],
        compiler_params=pltpu.CompilerParams(
            collective_id=0, has_side_effects=True, vmem_limit_bytes=48 << 20
        ),
    )(tile_count, tile_pos, tile_bits, edge_weight, syndrome, channel_prior, out_cot)


def finish(*parts):
    return pl.pallas_call(
        finish_kernel,
        out_shape=tuple(jax.ShapeDtypeStruct(part.shape, part.dtype) for part in parts),
        in_specs=[ANY_SPEC] * 3,
        out_specs=(ANY_SPEC,) * 3,
        scratch_shapes=[pltpu.SemaphoreType.DMA((3,))],
    )(*parts)


def body(*arguments):
    *parts, flag = sparse_parts(*arguments)
    return lax.cond(
        flag[0, 0] > 0.0,
        lambda given, kept: dense_body(*given),
        lambda given, kept: tuple(finish(*kept)),
        arguments,
        tuple(parts),
    )


def solution(mesh):
    placed = (
        P("chk", "var", None, None),
        P("chk", "var", None, None),
        P("chk", "var"),
        P("chk", "var", None, None),
        P("chk", None),
        P("var"),
        P("var", None),
    )
    return jax.shard_map(
        body,
        mesh=mesh,
        in_specs=placed,
        out_specs=(P("var", None), P("chk", "var", None, None), P("var")),
        check_vma=False,
    )
```
